512 devices in a mesh: row: 32 (over x, z), col: 16 (over y, core).
Axes of the slice: x: 4, y: 8, z: 8, core: 2. Of those that a mesh axis runs over, the one named last changes fastest.
Arguments:
- momentum: float32 [8192, 14336], P('row', 'col'), may hold values from -230 to 230
- gradient: bfloat16 [8192, 14336], P('row', 'col'), may hold values from -6 to 6
- right_basis: float32 [14336, 512], P('col', 'row'), may hold values from -6 to 6
Outputs:
- update: float32 [8192, 14336], P('row', 'col')
- new_momentum: float32 [8192, 14336], P('row', 'col')
- new_basis: float32 [14336, 512], P('col', 'row')
The draws below stay inside these ranges and needn't reach their ends.
All inputs are finite; a program needn't handle non-finite values.
Results may differ from the reference program's by a relative error of at most 0.0003.
Values sent between devices are 32-bit elements; how exact they have to be, the bound alone decides.
No kernel may reach another device: no remote copies, remote signals or barrier semaphores. Data moves between devices by JAX's collectives and lax.ppermute only.
A program may use at most 64 MiB of HBM per device.

```python
import math
import jax
import jax.numpy as jnp
from jax import lax

ROWS = 8192
COLS = 14336
RANK = 512


def draw_momentum(key, part):
    key = jax.random.fold_in(key, 11)
    key_rows, key_cols, key_base = jax.random.split(key, 3)
    row_pos = jnp.arange(ROWS, dtype=jnp.float32) / (ROWS - 1)
    col_pos = jnp.arange(COLS, dtype=jnp.float32) / (COLS - 1)
    row_scale = jnp.exp(row_pos * math.log(3.0) + jax.random.uniform(key_rows, (ROWS,), jnp.float32, -1.15, 1.15))
    col_scale = jnp.exp(col_pos * math.log(3.0) + jax.random.uniform(key_cols, (COLS,), jnp.float32, -1.15, 1.15))
    base = jnp.clip(jax.random.normal(key_base, (ROWS, COLS), jnp.float32), -5.0, 5.0)
    return (0.5 * base * row_scale[:, None] * col_scale[None, :]).astype(jnp.float32)


def shard_levels(rng, shape, cuts, smallest, top_value):
    def one(dim, shards_of):
        steps = jax.random.uniform(jax.random.fold_in(jax.random.fold_in(rng, 6), dim), (shards_of,), jnp.float32, smallest / len(cuts), top_value / len(cuts))
        return jnp.repeat(jnp.exp(steps), shape[dim] // shards_of).reshape((-1,) + (1,) * (len(shape) - dim - 1))

    loudness = one(*cuts[0])
    for cut in cuts[1:]:
        loudness = loudness * one(*cut)
    return loudness


def bell_draw(stream_key, shape, width, limit, cuts=(), kind=jnp.bfloat16):
    entries = jax.random.normal(stream_key, shape, jnp.float32) * width
    if len(cuts) > 0:
        entries = shard_levels(stream_key, shape, cuts, -0.22, 0.18) * entries
    return jnp.clip(entries, min=-limit, max=limit).astype(kind)


def setup_inputs(seed: int = 0) -> dict:
    splits = jax.random.split(jax.random.key(seed), 4)
    return {
        "momentum": draw_momentum(jax.random.fold_in(splits[3], 71), 0),
        "gradient": bell_draw(splits[1], (ROWS, COLS), 1.0, 6.0, ((0, 32), (1, 16))),
        "right_basis": bell_draw(splits[2], (COLS, RANK), 1.0, 6.0, ((0, 16), (1, 32)), jnp.float32),
    }


HIGH = lax.Precision.HIGHEST
epsilon_norm = 1e-06
retain = 0.7

def inner_rows(first, second):
    return lax.dot_general(first.astype(jnp.float32), second.astype(jnp.float32), (((0,), (0,)), ((), ())), precision=HIGH, preferred_element_type=jnp.float32)

def outer_cols(first, second):
    return lax.dot_general(first.astype(jnp.float32), second.astype(jnp.float32), (((1,), (1,)), ((), ())), precision=HIGH, preferred_element_type=jnp.float32)

def reference(momentum, gradient, right_basis):
    blended = momentum + gradient.astype(jnp.float32)
    left_factor = jnp.dot(blended.astype(jnp.float32), right_basis.astype(jnp.float32), precision=HIGH, preferred_element_type=jnp.float32)
    gram_matrix = inner_rows(left_factor, left_factor)
    chol_factor = jnp.linalg.cholesky(gram_matrix)
    orthonormal = jax.scipy.linalg.solve_triangular(chol_factor, left_factor.T, lower=True).T
    right_factor = inner_rows(blended, orthonormal)
    squares = lax.optimization_barrier(jnp.sum(right_factor * right_factor, axis=0))
    new_basis = right_factor / jnp.sqrt(squares + epsilon_norm)[None, :]
    new_momentum = blended - (1.0 - retain) * outer_cols(orthonormal, right_factor)
    scale = math.sqrt(ROWS * COLS / RANK)
    update = scale * outer_cols(orthonormal, new_basis)
    return (update, new_momentum, new_basis)
```

```python
import math

import jax
import jax.numpy as jnp
from jax import lax
from jax.experimental import pallas as pl
from jax.experimental.pallas import tpu as pltpu
from jax.sharding import PartitionSpec as P

ROWS = 8192
COLS = 14336
RANK = 512
BLOCK = 128
X, Y, Z, CORES = 4, 8, 8, 2


HIGH = lax.Precision.HIGH
HIGHEST = lax.Precision.HIGHEST
epsilon_norm = 1e-06
retain = 0.7


def dot(first, second, over, precision):
    return lax.dot_general(
        first, second, ((over[:1], over[1:]), ((), ())), precision=precision, preferred_element_type=jnp.float32
    )


def chips(way):
    upper = Z // 2
    row = lambda x, high, low: (x * upper + high) * 2 + low
    if way == "wide":
        return "row", [[row(x, high, low) for x in range(X) for low in range(2)] for high in range(upper)], 2 * X
    if way == "long":
        return "row", [[row(x, high, low) for high in range(upper)] for x in range(X) for low in range(2)], upper
    return "col", [[y * CORES + core for y in range(Y)] for core in range(CORES)], Y


def exchange(blocks, way):
    name, groups, _ = chips(way)
    return lax.all_to_all(blocks, name, 0, 0, axis_index_groups=groups, tiled=False)


def scatter_sum(whole, way):
    count = chips(way)[2]
    return jnp.sum(exchange(whole.reshape((count, whole.shape[0] // count) + whole.shape[1:]), way), axis=0)


def gather(part, way):
    count = chips(way)[2]
    return exchange(jnp.broadcast_to(part[None], (count,) + part.shape), way).reshape(
        (count * part.shape[0],) + part.shape[1:]
    )


def swap(part):
    return lax.ppermute(part, "col", [(i, i ^ 1) for i in range(Y * CORES)])


def halves(whole):
    half = whole.shape[0] // CORES
    core = lax.axis_index("col") % CORES
    return (
        lax.dynamic_slice_in_dim(whole, core * half, half, 0),
        lax.dynamic_slice_in_dim(whole, (1 - core) * half, half, 0),
    )


def join(own, other):
    first = lax.axis_index("col") % CORES == 0
    return jnp.concatenate([jnp.where(first, own, other), jnp.where(first, other, own)], axis=0)


def split(value):
    high = value.astype(jnp.bfloat16)
    return high, (value - high.astype(jnp.float32)).astype(jnp.bfloat16)


def dot3(first, second, over):
    one = lambda a, b: lax.dot_general(
        a, b, ((over[:1], over[1:]), ((), ())), preferred_element_type=jnp.float32
    )
    return one(first[0], second[0]) + (one(first[0], second[1]) + one(first[1], second[0]))


def products_kernel(left_ref, blended_ref, out_ref):
    half = left_ref.shape[0] // 2
    cols = blended_ref.shape[1]
    top, low = left_ref[:half, :], left_ref[half:, :]
    out_ref[:, :cols] = dot3(split(left_ref[...]), split(blended_ref[...]), (1, 0))
    out_ref[:half, cols : cols + half] = dot(top, top, (1, 1), HIGHEST)
    out_ref[half:, cols : cols + half] = dot(low, low, (1, 1), HIGHEST)
    across = dot(top, low, (1, 1), HIGHEST)
    out_ref[:half, cols + half :] = across[:, : half // 2]
    out_ref[half:, cols + half :] = across[:, half // 2 :]


def products(left, blended):
    rank, cols = left.shape[0], blended.shape[1]
    return pl.pallas_call(
        products_kernel,
        out_shape=jax.ShapeDtypeStruct((rank, cols + 3 * rank // 4), jnp.float32),
        in_specs=[pl.BlockSpec(memory_space=pltpu.VMEM)] * 2,
        out_specs=pl.BlockSpec(memory_space=pltpu.VMEM),
        compiler_params=pltpu.CompilerParams(vmem_limit_bytes=32 * 2**20),
        cost_estimate=pl.CostEstimate(flops=2 * 10**9, bytes_accessed=2 * 2**20, transcendentals=0),
        name="products",
    )(left, blended)


def invert_block(block):
    groups = BLOCK // 8
    sub = lax.broadcasted_iota(jnp.int32, (8, BLOCK), 0)
    lane = lax.broadcasted_iota(jnp.int32, (8, BLOCK), 1)
    work = [block[8 * q : 8 * q + 8, :] for q in range(groups)]
    side = [jnp.where(lane == sub + 8 * q, 1.0, 0.0).astype(jnp.float32) for q in range(groups)]
    out = []
    for p in range(groups):
        spread = {
            q: [jnp.broadcast_to(work[q][:, 8 * p + j : 8 * p + j + 1], (8, BLOCK)) for j in range(8)]
            for q in range(p, groups)
        }
        pivots = jnp.ones((8, BLOCK), jnp.float32)
        for j in range(8):
            row = [jnp.broadcast_to(spread[p][k][j : j + 1, :], (8, BLOCK)) for k in range(j, 8)]
            pivots = jnp.where(sub == j, row[0], pivots)
            inverse = 1.0 / row[0]
            row_work = jnp.broadcast_to(work[p][j : j + 1, :], (8, BLOCK))
            row_side = jnp.broadcast_to(side[p][j : j + 1, :], (8, BLOCK))
            for q in range(p, groups):
                times = spread[q][j] * inverse
                if q == p:
                    times = jnp.where(sub > j, times, 0.0)
                for k in range(j + 1, 8):
                    spread[q][k] = spread[q][k] - times * row[k - j]
                work[q] = work[q] - times * row_work
                side[q] = side[q] - times * row_side
        out.append(side[p] * lax.rsqrt(pivots))
    return jnp.concatenate(out, axis=0)


def factor_kernel(gram_ref, out_ref, work):
    rank = gram_ref.shape[0]
    half = rank // 2
    count = rank // BLOCK
    work[:half, : half + half // 2] = gram_ref[:half, :]
    work[half:, :half] = jnp.zeros((half, half), jnp.float32)
    work[half:, half:] = gram_ref[half:, :half]
    work[:half, half + half // 2 :] = gram_ref[half:, half:]
    rows = lax.broadcasted_iota(jnp.int32, (rank, rank), 0)
    cols = lax.broadcasted_iota(jnp.int32, (rank, rank), 1)
    out_ref[...] = jnp.where(rows == cols, 1.0, 0.0)

    def step(k, carry):
        at = pl.ds(pl.multiple_of(k * BLOCK, BLOCK), BLOCK)
        inverse = invert_block(work[at, at])
        upper = dot(inverse, work[at, :], (1, 0), HIGHEST)
        side = dot(inverse, out_ref[at, :], (1, 0), HIGHEST)
        out_ref[at, :] = side
        for i in range(1, count):

            @pl.when(i > k)
            def _():
                below = pl.ds(i * BLOCK, BLOCK)
                times = upper[:, i * BLOCK : (i + 1) * BLOCK]
                work[below, :] -= dot(times, upper, (0, 0), HIGHEST)
                out_ref[below, :] -= dot(times, side, (0, 0), HIGHEST)

        return carry

    lax.fori_loop(0, count, step, 0)


def inverse_factor(gram_matrix):
    rank = gram_matrix.shape[0]
    return pl.pallas_call(
        factor_kernel,
        out_shape=jax.ShapeDtypeStruct((rank, rank), jnp.float32),
        in_specs=[pl.BlockSpec(memory_space=pltpu.VMEM)],
        out_specs=pl.BlockSpec(memory_space=pltpu.VMEM),
        scratch_shapes=[pltpu.VMEM((rank, rank), jnp.float32)],
        compiler_params=pltpu.CompilerParams(vmem_limit_bytes=16 * 2**20),
        cost_estimate=pl.CostEstimate(flops=2 * 10**9, bytes_accessed=2 * 2**20, transcendentals=0),
        name="inverse_factor",
    )(gram_matrix)


def right_kernel(inverse_ref, raw_ref, left_ref, right_ref, ortho_ref, squares_ref):
    rank = inverse_ref.shape[0]
    raw, left = split(raw_ref[...]), split(left_ref[...])
    eye = lax.broadcasted_iota(jnp.int32, (BLOCK, BLOCK), 0) == lax.broadcasted_iota(jnp.int32, (BLOCK, BLOCK), 1)
    for i in range(rank // BLOCK):
        at, upto = pl.ds(i * BLOCK, BLOCK), (i + 1) * BLOCK
        inverse = split(inverse_ref[at, :upto])
        right = dot3(inverse, [part[:upto] for part in raw], (1, 0))
        right_ref[at, :] = right
        ortho_ref[at, :] = dot3(inverse, [part[:upto] for part in left], (1, 0))
        sums = jnp.sum(right * right, axis=1, keepdims=True)
        squares_ref[pl.ds(i, 1), :] = jnp.sum(jnp.where(eye, sums, 0.0), axis=0, keepdims=True)


def momentum_kernel(blended_ref, ortho_ref, right_ref, out_ref):
    out_ref[...] = blended_ref[...] - (1.0 - retain) * dot3(split(ortho_ref[...]), split(right_ref[...]), (0, 0))


def update_kernel(start_ref, squares_ref, ortho_ref, right_ref, update_ref, basis_ref, scaled):
    scale = math.sqrt(ROWS * COLS / RANK)
    rank, width = ortho_ref.shape[0], basis_ref.shape[0]
    rows = jnp.sum(squares_ref[...], axis=0)
    factors = lax.rsqrt(rows + epsilon_norm)
    eye = lax.broadcasted_iota(jnp.int32, (BLOCK, BLOCK), 0) == lax.broadcasted_iota(jnp.int32, (BLOCK, BLOCK), 1)
    for i in range(rank // BLOCK):
        at = pl.ds(i * BLOCK, BLOCK)
        column = jnp.sum(jnp.where(eye, factors[i : i + 1, :], 0.0), axis=1, keepdims=True)
        scaled[at, :] = jnp.broadcast_to(column, (BLOCK, BLOCK))
    ortho = ortho_ref[...] * (scale * scaled[:, :1])
    update_ref[...] = dot3(split(ortho), split(right_ref[...]), (0, 0))
    own = pl.ds(pl.multiple_of(start_ref[0], width), width)
    basis_ref[...] = right_ref[own, :] * scaled[own, :1]


VMEM = pl.BlockSpec(memory_space=pltpu.VMEM)


def call(kernel, name, shapes, specs, flops, *operands, scratch=()):
    return pl.pallas_call(
        kernel,
        out_shape=[jax.ShapeDtypeStruct(shape, jnp.float32) for shape in shapes],
        in_specs=specs,
        out_specs=[VMEM] * len(shapes),
        scratch_shapes=list(scratch),
        compiler_params=pltpu.CompilerParams(vmem_limit_bytes=32 * 2**20),
        cost_estimate=pl.CostEstimate(flops=flops, bytes_accessed=4 * 2**20, transcendentals=0),
        name=name,
    )(*operands)


def body(momentum, gradient, right_basis):
    rank = right_basis.shape[1] * lax.axis_size("row")
    scale = math.sqrt(ROWS * COLS / RANK)
    with jax.named_scope("basis_gather"):
        basis = gather(gather(right_basis.T, "long"), "wide")
    blended = momentum + gradient.astype(jnp.float32)
    with jax.named_scope("left"):
        left_own, left_other = halves(dot(basis, blended, (1, 1), HIGH))
        left_own = gather(scatter_sum(left_own + swap(left_other), "y"), "y")
        left = join(left_own, swap(left_own)).reshape(X, 2, Z // 2, -1, blended.shape[0])
        left = left.transpose(0, 2, 1, 3, 4).reshape(rank, blended.shape[0])
    with jax.named_scope("sums"):
        cols = blended.shape[1]
        sums = gather(scatter_sum(scatter_sum(products(left, blended), "wide"), "long"), "long")
        gram_matrix = gather(sums[:, cols:], "wide")
        right_raw = gather(sums[:, :cols], "wide")
    with jax.named_scope("factor"):
        inverse = inverse_factor(gram_matrix)
    rows = blended.shape[0]
    width = right_basis.shape[1]
    with jax.named_scope("right"):
        right, ortho, squares = call(
            right_kernel,
            "right",
            [(rank, cols), (rank, rows), (rank // BLOCK, BLOCK)],
            [VMEM] * 3,
            2 * 10**9,
            inverse,
            right_raw,
            left,
        )
    with jax.named_scope("squares"):
        peers = lax.axis_size("col")
        squares = lax.all_to_all(jnp.broadcast_to(squares[None], (peers,) + squares.shape), "col", 0, 0, tiled=False)
    with jax.named_scope("outputs"):
        (new_momentum,) = call(
            momentum_kernel, "momentum", [(rows, cols)], [VMEM] * 3, 10**9, blended, ortho, right
        )
        start = (lax.axis_index("row") * width).astype(jnp.int32).reshape(1)
        update, new_basis = call(
            update_kernel,
            "update",
            [(rows, cols), (width, cols)],
            [pl.BlockSpec(memory_space=pltpu.SMEM)] + [VMEM] * 3,
            10**9,
            start,
            squares,
            ortho,
            right,
            scratch=[pltpu.VMEM((rank, BLOCK), jnp.float32)],
        )
        new_basis = new_basis.T
    return (update, new_momentum, new_basis)


def solution(mesh):
    in_specs = (P("row", "col"), P("row", "col"), P("col", "row"))
    out_specs = (P("row", "col"), P("row", "col"), P("col", "row"))
    return jax.shard_map(body, mesh=mesh, in_specs=in_specs, out_specs=out_specs, check_vma=False)
```

```python
import math

import jax
import jax.numpy as jnp
from jax import lax
from jax.experimental import pallas as pl
from jax.experimental.pallas import tpu as pltpu
from jax.sharding import PartitionSpec as P

ROWS = 8192
COLS = 14336
RANK = 512
BLOCK = 128
X, Y, Z, CORES = 4, 8, 8, 2
CORE_BLOCKS = (
    ((0, 0), (0, 1), (0, 2), (0, 3), (1, 1)),
    ((1, 2), (1, 3), (2, 2), (2, 3), (3, 3)),
)


HIGH = lax.Precision.HIGH
HIGHEST = lax.Precision.HIGHEST
epsilon_norm = 1e-06
retain = 0.7


def dot(first, second, over, precision):
    return lax.dot_general(
        first, second, ((over[:1], over[1:]), ((), ())), precision=precision, preferred_element_type=jnp.float32
    )


def chips(way):
    upper = Z // 2
    row = lambda x, high, low: (x * upper + high) * 2 + low
    if way == "wide":
        return "row", [[row(x, high, low) for x in range(X) for low in range(2)] for high in range(upper)], 2 * X
    if way == "long":
        return "row", [[row(x, high, low) for high in range(upper)] for x in range(X) for low in range(2)], upper
    return "col", [[y * CORES + core for y in range(Y)] for core in range(CORES)], Y


def exchange(blocks, way):
    name, groups, _ = chips(way)
    return lax.all_to_all(blocks, name, 0, 0, axis_index_groups=groups, tiled=False)


def scatter_sum(blocks, way):
    return jnp.sum(exchange(blocks, way), axis=0)


def copies(part, way):
    return jnp.broadcast_to(part[None], (chips(way)[2],) + part.shape)


def gather(part, way):
    return exchange(copies(part, way), way)


def swap(part):
    return lax.ppermute(part, "col", [(i, i ^ 1) for i in range(Y * CORES)])


def halves(whole):
    half = whole.shape[0] // CORES
    core = lax.axis_index("col") % CORES
    return (
        lax.dynamic_slice_in_dim(whole, core * half, half, 0),
        lax.dynamic_slice_in_dim(whole, (1 - core) * half, half, 0),
    )


def join(own, other):
    first = lax.axis_index("col") % CORES == 0
    return jnp.concatenate([jnp.where(first, own, other), jnp.where(first, other, own)], axis=0)


def split(value):
    high = value.astype(jnp.bfloat16)
    return high, (value - high.astype(jnp.float32)).astype(jnp.bfloat16)


def dot3(first, second, over):
    one = lambda a, b: lax.dot_general(
        a, b, ((over[:1], over[1:]), ((), ())), preferred_element_type=jnp.float32
    )
    return one(first[0], second[0]) + (one(first[0], second[1]) + one(first[1], second[0]))


def square(k):
    return pl.ds(k * BLOCK, BLOCK)


def products_kernel(core_ref, left_ref, blended_ref, out_ref):
    members, uppers = out_ref.shape[:2]
    deep = left_ref.shape[0] // (8 * members * uppers)
    lanes = blended_ref.shape[1] // BLOCK
    right = dot3(split(left_ref[...]), split(blended_ref[...]), (1, 0))
    for j in range(lanes):
        tiles = right[:, j * BLOCK : (j + 1) * BLOCK].reshape(members, uppers, deep, 8, BLOCK)
        for i in range(deep):
            out_ref[:, :, i * lanes + j] = tiles[:, :, i]

    def gram(blocks):
        found = [dot(left_ref[square(k), :], left_ref[square(l), :], (1, 1), HIGHEST) for k, l in blocks]
        found.append(jnp.zeros((BLOCK, BLOCK), jnp.float32))
        for t in range(len(found) // 2):
            pair = jnp.concatenate(found[2 * t : 2 * t + 2], axis=0)
            out_ref[:, :, deep * lanes + t] = pair.reshape(members, uppers, 8, BLOCK)

    pl.when(core_ref[0] == 0)(lambda: gram(CORE_BLOCKS[0]))
    pl.when(core_ref[0] != 0)(lambda: gram(CORE_BLOCKS[1]))


def copies_kernel(sums_ref, out_ref):
    members, rows, cols = out_ref.shape
    uppers = sums_ref.shape[0]
    deep, lanes = rows // (8 * uppers), cols // BLOCK
    for j in range(lanes):
        tiles = [sums_ref[:, i * lanes + j] for i in range(deep)]
        piece = jnp.stack(tiles, axis=1).reshape(rows, BLOCK)
        for member in range(members):
            out_ref[member, :, j * BLOCK : (j + 1) * BLOCK] = piece


def invert_block(block):
    groups = BLOCK // 8
    sub = lax.broadcasted_iota(jnp.int32, (8, BLOCK), 0)
    lane = lax.broadcasted_iota(jnp.int32, (8, BLOCK), 1)
    work = [block[8 * q : 8 * q + 8, :] for q in range(groups)]
    side = [jnp.where(lane == sub + 8 * q, 1.0, 0.0).astype(jnp.float32) for q in range(groups)]
    out = []
    for p in range(groups):
        spread = {
            q: [jnp.broadcast_to(work[q][:, 8 * p + j : 8 * p + j + 1], (8, BLOCK)) for j in range(8)]
            for q in range(p, groups)
        }
        pivots = jnp.ones((8, BLOCK), jnp.float32)
        for j in range(8):
            row = [jnp.broadcast_to(spread[p][k][j : j + 1, :], (8, BLOCK)) for k in range(j, 8)]
            pivots = jnp.where(sub == j, row[0], pivots)
            inverse = 1.0 / row[0]
            row_work = jnp.broadcast_to(work[p][j : j + 1, :], (8, BLOCK))
            row_side = jnp.broadcast_to(side[p][j : j + 1, :], (8, BLOCK))
            for q in range(p, groups):
                times = spread[q][j] * inverse
                if q == p:
                    times = jnp.where(sub > j, times, 0.0)
                for k in range(j + 1, 8):
                    spread[q][k] = spread[q][k] - times * row[k - j]
                work[q] = work[q] - times * row_work
                side[q] = side[q] - times * row_side
        out.append(side[p] * lax.rsqrt(pivots))
    return jnp.concatenate(out, axis=0)


def factor_kernel(core_ref, own_ref, other_ref, out_ref, work):
    rank = out_ref.shape[0]
    count = rank // BLOCK
    work[...] = jnp.zeros((rank, rank), jnp.float32)

    def place(parts):
        for part_ref, blocks in zip(parts, CORE_BLOCKS):
            half = part_ref.shape[0] // 2
            for i, (k, l) in enumerate(blocks):
                tiles = part_ref[i % 2 * half : (i % 2 + 1) * half, :, i // 2]
                work[square(k), square(l)] = tiles.reshape(BLOCK, BLOCK)

    pl.when(core_ref[0] == 0)(lambda: place((own_ref, other_ref)))
    pl.when(core_ref[0] != 0)(lambda: place((other_ref, own_ref)))
    rows = lax.broadcasted_iota(jnp.int32, (rank, rank), 0)
    cols = lax.broadcasted_iota(jnp.int32, (rank, rank), 1)
    out_ref[...] = jnp.where(rows == cols, 1.0, 0.0)

    def step(k, carry):
        at = pl.ds(pl.multiple_of(k * BLOCK, BLOCK), BLOCK)
        inverse = invert_block(work[at, at])
        upper = dot(inverse, work[at, :], (1, 0), HIGHEST)
        side = dot(inverse, out_ref[at, :], (1, 0), HIGHEST)
        out_ref[at, :] = side
        for i in range(1, count):

            @pl.when(i > k)
            def _():
                below = pl.ds(i * BLOCK, BLOCK)
                times = upper[:, i * BLOCK : (i + 1) * BLOCK]
                work[below, :] -= dot(times, upper, (0, 0), HIGHEST)
                out_ref[below, :] -= dot(times, side, (0, 0), HIGHEST)

        return carry

    lax.fori_loop(0, count, step, 0)


def right_kernel(inverse_ref, raw_ref, left_ref, right_ref, ortho_ref, squares_ref):
    rank = inverse_ref.shape[0]
    raw, left = split(raw_ref[...]), split(left_ref[...])
    eye = lax.broadcasted_iota(jnp.int32, (BLOCK, BLOCK), 0) == lax.broadcasted_iota(jnp.int32, (BLOCK, BLOCK), 1)
    for i in range(rank // BLOCK):
        at, upto = pl.ds(i * BLOCK, BLOCK), (i + 1) * BLOCK
        inverse = split(inverse_ref[at, :upto])
        right = dot3(inverse, [part[:upto] for part in raw], (1, 0))
        right_ref[at, :] = right
        ortho_ref[at, :] = dot3(inverse, [part[:upto] for part in left], (1, 0))
        sums = jnp.sum(right * right, axis=1, keepdims=True)
        squares_ref[pl.ds(i, 1), :] = jnp.sum(jnp.where(eye, sums, 0.0), axis=0, keepdims=True)


def momentum_kernel(blended_ref, ortho_ref, right_ref, out_ref):
    out_ref[...] = blended_ref[...] - (1.0 - retain) * dot3(split(ortho_ref[...]), split(right_ref[...]), (0, 0))


def update_kernel(start_ref, squares_ref, ortho_ref, right_ref, update_ref, basis_ref, scaled):
    scale = math.sqrt(ROWS * COLS / RANK)
    rank, width = ortho_ref.shape[0], basis_ref.shape[0]
    rows = jnp.sum(squares_ref[...], axis=0)
    factors = lax.rsqrt(rows + epsilon_norm)
    eye = lax.broadcasted_iota(jnp.int32, (BLOCK, BLOCK), 0) == lax.broadcasted_iota(jnp.int32, (BLOCK, BLOCK), 1)
    for i in range(rank // BLOCK):
        at = pl.ds(i * BLOCK, BLOCK)
        column = jnp.sum(jnp.where(eye, factors[i : i + 1, :], 0.0), axis=1, keepdims=True)
        scaled[at, :] = jnp.broadcast_to(column, (BLOCK, BLOCK))
    ortho = ortho_ref[...] * (scale * scaled[:, :1])
    update_ref[...] = dot3(split(ortho), split(right_ref[...]), (0, 0))
    own = pl.ds(pl.multiple_of(start_ref[0], width), width)
    basis_ref[...] = right_ref[own, :] * scaled[own, :1]


VMEM = pl.BlockSpec(memory_space=pltpu.VMEM)
SMEM = pl.BlockSpec(memory_space=pltpu.SMEM)


def call(kernel, name, shapes, flops, *operands, scratch=(), limit=10):
    return pl.pallas_call(
        kernel,
        out_shape=[jax.ShapeDtypeStruct(shape, jnp.float32) for shape in shapes],
        in_specs=[SMEM if operand.dtype == jnp.int32 else VMEM for operand in operands],
        out_specs=[VMEM] * len(shapes),
        scratch_shapes=list(scratch),
        compiler_params=pltpu.CompilerParams(vmem_limit_bytes=limit * 2**20),
        cost_estimate=pl.CostEstimate(flops=flops, bytes_accessed=4 * 2**20, transcendentals=0),
        name=name,
    )(*operands)


def body(momentum, gradient, right_basis):
    cols, width = right_basis.shape
    rows = momentum.shape[0]
    rank = width * lax.axis_size("row")
    members, uppers = chips("wide")[2], chips("long")[2]
    core = (lax.axis_index("col") % CORES).astype(jnp.int32).reshape(1)
    with jax.named_scope("basis_gather"):
        basis = gather(gather(right_basis.T, "long"), "wide").reshape(rank, cols)
    blended = momentum + gradient.astype(jnp.float32)
    with jax.named_scope("left"):
        left_own, left_other = halves(dot(basis, blended, (1, 1), HIGH))
        left_own = left_own + swap(left_other)
        left_own = gather(scatter_sum(left_own.reshape(Y, -1, rows), "y"), "y").reshape(-1, rows)
        left = join(left_own, swap(left_own)).reshape(X, 2, uppers, width, rows)
        left = left.transpose(0, 2, 1, 3, 4).reshape(rank, rows)
    with jax.named_scope("sums"):
        tiles = width // 8 * (cols // BLOCK)
        per_core = (len(CORE_BLOCKS[0]) + 1) // 2
        shape = (members, uppers, tiles + per_core, 8, BLOCK)
        (sums,) = call(products_kernel, "products", [shape], 2 * 10**9, core, left, blended)
        sums = gather(scatter_sum(scatter_sum(sums, "wide"), "long"), "long")
        gram_own = gather(sums[:, tiles:], "wide")
        (raw,) = call(copies_kernel, "copies", [(members, rank // members, cols)], 10**6, sums)
        gram_own, raw = lax.optimization_barrier((gram_own, raw))
        gram_other = swap(gram_own)
        right_raw = exchange(raw, "wide").reshape(rank, cols)
    with jax.named_scope("factor"):
        (inverse,) = call(
            factor_kernel,
            "inverse_factor",
            [(rank, rank)],
            2 * 10**9,
            core,
            gram_own,
            gram_other,
            scratch=[pltpu.VMEM((rank, rank), jnp.float32)],
        )
    with jax.named_scope("right"):
        shapes = [(rank, cols), (rank, rows), (rank // BLOCK, BLOCK)]
        right, ortho, squares = call(right_kernel, "right", shapes, 2 * 10**9, inverse, right_raw, left)
    with jax.named_scope("squares"):
        squares = jnp.broadcast_to(squares[None], (lax.axis_size("col"),) + squares.shape)
        squares = lax.all_to_all(squares, "col", 0, 0, tiled=False)
    with jax.named_scope("outputs"):
        (new_momentum,) = call(momentum_kernel, "momentum", [(rows, cols)], 10**9, blended, ortho, right)
        start = (lax.axis_index("row") * width).astype(jnp.int32).reshape(1)
        shapes = [(rows, cols), (width, cols)]
        scratch = [pltpu.VMEM((rank, BLOCK), jnp.float32)]
        update, new_basis = call(
            update_kernel, "update", shapes, 10**9, start, squares, ortho, right, scratch=scratch
        )
        new_basis = new_basis.T
    return (update, new_momentum, new_basis)


def solution(mesh):
    in_specs = (P("row", "col"), P("row", "col"), P("col", "row"))
    out_specs = (P("row", "col"), P("row", "col"), P("col", "row"))
    return jax.shard_map(body, mesh=mesh, in_specs=in_specs, out_specs=out_specs, check_vma=False)
```

```python
import math

import jax
import jax.numpy as jnp
from jax import lax
from jax.experimental import pallas as pl
from jax.experimental.pallas import tpu as pltpu
from jax.sharding import PartitionSpec as P

ROWS = 8192
COLS = 14336
RANK = 512
BLOCK = 128
X, Y, Z, CORES = 4, 8, 8, 2
CORE_BLOCKS = (
    ((0, 0), (0, 1), (0, 2), (0, 3), (1, 1)),
    ((1, 2), (1, 3), (2, 2), (2, 3), (3, 3)),
)


HIGH = lax.Precision.HIGH
HIGHEST = lax.Precision.HIGHEST
epsilon_norm = 1e-06
retain = 0.7


def dot(first, second, over, precision):
    return lax.dot_general(
        first, second, ((over[:1], over[1:]), ((), ())), precision=precision, preferred_element_type=jnp.float32
    )


def chips(way):
    upper = Z // 2
    row = lambda x, high, low: (x * upper + high) * 2 + low
    if way == "wide":
        return "row", [[row(x, high, low) for x in range(X) for low in range(2)] for high in range(upper)], 2 * X
    if way == "long":
        return "row", [[row(x, high, low) for high in range(upper)] for x in range(X) for low in range(2)], upper
    return "col", [[y * CORES + core for y in range(Y)] for core in range(CORES)], Y


def exchange(blocks, way):
    name, groups, _ = chips(way)
    return lax.all_to_all(blocks, name, 0, 0, axis_index_groups=groups, tiled=False)


def scatter_sum(blocks, way):
    return jnp.sum(exchange(blocks, way), axis=0)


def copies(part, way):
    return jnp.broadcast_to(part[None], (chips(way)[2],) + part.shape)


def gather(part, way):
    return exchange(copies(part, way), way)


def swap(part):
    return lax.ppermute(part, "col", [(i, i ^ 1) for i in range(Y * CORES)])


def halves(whole):
    half = whole.shape[0] // CORES
    core = lax.axis_index("col") % CORES
    return (
        lax.dynamic_slice_in_dim(whole, core * half, half, 0),
        lax.dynamic_slice_in_dim(whole, (1 - core) * half, half, 0),
    )


def join(own, other):
    first = lax.axis_index("col") % CORES == 0
    return jnp.concatenate([jnp.where(first, own, other), jnp.where(first, other, own)], axis=0)


def split(value):
    high = value.astype(jnp.bfloat16)
    return high, (value - high.astype(jnp.float32)).astype(jnp.bfloat16)


def dot3(first, second, over):
    one = lambda a, b: lax.dot_general(
        a, b, ((over[:1], over[1:]), ((), ())), preferred_element_type=jnp.float32
    )
    return one(first[0], second[0]) + (one(first[0], second[1]) + one(first[1], second[0]))


def square(k):
    return pl.ds(k * BLOCK, BLOCK)


def products_kernel(core_ref, left_ref, blended_ref, out_ref):
    members, uppers = out_ref.shape[:2]
    deep = left_ref.shape[0] // (8 * members * uppers)
    lanes = blended_ref.shape[1] // BLOCK
    right = dot3(split(left_ref[...]), split(blended_ref[...]), (1, 0))
    for j in range(lanes):
        tiles = right[:, j * BLOCK : (j + 1) * BLOCK].reshape(members, uppers, deep, 8, BLOCK)
        for i in range(deep):
            out_ref[:, :, i * lanes + j] = tiles[:, :, i]

    def gram(blocks):
        found = [dot(left_ref[square(k), :], left_ref[square(l), :], (1, 1), HIGHEST) for k, l in blocks]
        found.append(jnp.zeros((BLOCK, BLOCK), jnp.float32))
        for t in range(len(found) // 2):
            pair = jnp.concatenate(found[2 * t : 2 * t + 2], axis=0)
            out_ref[:, :, deep * lanes + t] = pair.reshape(members, uppers, 8, BLOCK)

    pl.when(core_ref[0] == 0)(lambda: gram(CORE_BLOCKS[0]))
    pl.when(core_ref[0] != 0)(lambda: gram(CORE_BLOCKS[1]))


def copies_kernel(sums_ref, out_ref):
    members, rows, cols = out_ref.shape
    uppers = sums_ref.shape[0]
    deep, lanes = rows // (8 * uppers), cols // BLOCK
    for j in range(lanes):
        tiles = [sums_ref[:, i * lanes + j] for i in range(deep)]
        piece = jnp.stack(tiles, axis=1).reshape(rows, BLOCK)
        for member in range(members):
            out_ref[member, :, j * BLOCK : (j + 1) * BLOCK] = piece


def invert_block(block):
    groups = BLOCK // 8
    sub = lax.broadcasted_iota(jnp.int32, (8, BLOCK), 0)
    lane = lax.broadcasted_iota(jnp.int32, (8, BLOCK), 1)
    work = [block[8 * q : 8 * q + 8, :] for q in range(groups)]
    side = [jnp.where(lane == sub + 8 * q, 1.0, 0.0).astype(jnp.float32) for q in range(groups)]
    out = []
    for p in range(groups):
        spread = {
            q: [jnp.broadcast_to(work[q][:, 8 * p + j : 8 * p + j + 1], (8, BLOCK)) for j in range(8)]
            for q in range(p, groups)
        }
        pivots = jnp.ones((8, BLOCK), jnp.float32)
        for j in range(8):
            row = [jnp.broadcast_to(spread[p][k][j : j + 1, :], (8, BLOCK)) for k in range(j, 8)]
            pivots = jnp.where(sub == j, row[0], pivots)
            inverse = 1.0 / row[0]
            row_work = jnp.broadcast_to(work[p][j : j + 1, :], (8, BLOCK))
            row_side = jnp.broadcast_to(side[p][j : j + 1, :], (8, BLOCK))
            for q in range(p, groups):
                times = spread[q][j] * inverse
                if q == p:
                    times = jnp.where(sub > j, times, 0.0)
                for k in range(j + 1, 8):
                    spread[q][k] = spread[q][k] - times * row[k - j]
                work[q] = work[q] - times * row_work
                side[q] = side[q] - times * row_side
        out.append(side[p] * lax.rsqrt(pivots))
    return jnp.concatenate(out, axis=0)


def factor_kernel(core_ref, own_hbm, other_hbm, out_hbm, own_ref, other_ref, out_ref, work, sems):
    rank = out_ref.shape[0]
    count = rank // BLOCK
    arrive = [
        pltpu.make_async_copy(own_hbm, own_ref, sems.at[0]),
        pltpu.make_async_copy(other_hbm, other_ref, sems.at[1]),
    ]
    for part in arrive:
        part.start()
    work[...] = jnp.zeros((rank, rank), jnp.float32)

    def place(parts):
        for part_ref, blocks in zip(parts, CORE_BLOCKS):
            half = part_ref.shape[0] // 2
            for i, (k, l) in enumerate(blocks):
                tiles = part_ref[i % 2 * half : (i % 2 + 1) * half, :, i // 2]
                work[square(k), square(l)] = tiles.reshape(BLOCK, BLOCK)

    for part in arrive:
        part.wait()
    pl.when(core_ref[0] == 0)(lambda: place((own_ref, other_ref)))
    pl.when(core_ref[0] != 0)(lambda: place((other_ref, own_ref)))
    rows = lax.broadcasted_iota(jnp.int32, (rank, rank), 0)
    cols = lax.broadcasted_iota(jnp.int32, (rank, rank), 1)
    out_ref[...] = jnp.where(rows == cols, 1.0, 0.0)

    def step(k, carry):
        at = pl.ds(pl.multiple_of(k * BLOCK, BLOCK), BLOCK)
        inverse = invert_block(work[at, at])
        upper = dot(inverse, work[at, :], (1, 0), HIGHEST)
        side = dot(inverse, out_ref[at, :], (1, 0), HIGHEST)
        out_ref[at, :] = side
        for i in range(1, count):

            @pl.when(i > k)
            def _():
                below = pl.ds(i * BLOCK, BLOCK)
                times = upper[:, i * BLOCK : (i + 1) * BLOCK]
                work[below, :] -= dot(times, upper, (0, 0), HIGHEST)
                out_ref[below, :] -= dot(times, side, (0, 0), HIGHEST)

        return carry

    lax.fori_loop(0, count, step, 0)
    leave = pltpu.make_async_copy(out_ref, out_hbm, sems.at[2])
    leave.start()
    leave.wait()


def right_kernel(
    inverse_hbm, raw_ref, left_ref, right_hbm, ortho_hbm, squares_ref, inverse_ref, right_ref, ortho_ref, arrive, leave
):
    count = raw_ref.shape[0] // BLOCK
    blocks = [pltpu.make_async_copy(inverse_hbm.at[square(i)], inverse_ref.at[square(i)], arrive.at[i]) for i in range(count)]
    for block in blocks:
        block.start()
    raw, left = split(raw_ref[...]), split(left_ref[...])
    eye = lax.broadcasted_iota(jnp.int32, (BLOCK, BLOCK), 0) == lax.broadcasted_iota(jnp.int32, (BLOCK, BLOCK), 1)
    out = []
    for i in range(count):
        at, upto = square(i), (i + 1) * BLOCK
        blocks[i].wait()
        inverse = split(inverse_ref[at, :upto])
        right = dot3(inverse, [part[:upto] for part in raw], (1, 0))
        right_ref[at, :] = right
        ortho_ref[at, :] = dot3(inverse, [part[:upto] for part in left], (1, 0))
        out.append(pltpu.make_async_copy(right_ref.at[at], right_hbm.at[at], leave.at[0, i]))
        out.append(pltpu.make_async_copy(ortho_ref.at[at], ortho_hbm.at[at], leave.at[1, i]))
        out[-2].start()
        out[-1].start()
        sums = jnp.sum(right * right, axis=1, keepdims=True)
        squares_ref[pl.ds(i, 1), :] = jnp.sum(jnp.where(eye, sums, 0.0), axis=0, keepdims=True)
    for block in out:
        block.wait()


def momentum_kernel(blended_ref, ortho_ref, right_ref, out_ref):
    out_ref[...] = blended_ref[...] - (1.0 - retain) * dot3(split(ortho_ref[...]), split(right_ref[...]), (0, 0))


def update_kernel(start_ref, squares_ref, ortho_ref, right_ref, update_ref, basis_ref, scaled):
    scale = math.sqrt(ROWS * COLS / RANK)
    rank, width = ortho_ref.shape[0], basis_ref.shape[0]
    rows = jnp.sum(squares_ref[...], axis=0)
    factors = lax.rsqrt(rows + epsilon_norm)
    eye = lax.broadcasted_iota(jnp.int32, (BLOCK, BLOCK), 0) == lax.broadcasted_iota(jnp.int32, (BLOCK, BLOCK), 1)
    for i in range(rank // BLOCK):
        at = pl.ds(i * BLOCK, BLOCK)
        column = jnp.sum(jnp.where(eye, factors[i : i + 1, :], 0.0), axis=1, keepdims=True)
        scaled[at, :] = jnp.broadcast_to(column, (BLOCK, BLOCK))
    ortho = ortho_ref[...] * (scale * scaled[:, :1])
    update_ref[...] = dot3(split(ortho), split(right_ref[...]), (0, 0))
    own = pl.ds(pl.multiple_of(start_ref[0], width), width)
    basis_ref[...] = right_ref[own, :] * scaled[own, :1]


VMEM = pl.BlockSpec(memory_space=pltpu.VMEM)
SMEM = pl.BlockSpec(memory_space=pltpu.SMEM)
HBM = pl.BlockSpec(memory_space=pltpu.HBM)


def call(kernel, name, shapes, flops, *operands, scratch=(), limit=10, takes=(), gives=()):
    return pl.pallas_call(
        kernel,
        out_shape=[jax.ShapeDtypeStruct(shape, jnp.float32) for shape in shapes],
        in_specs=[
            SMEM if operand.dtype == jnp.int32 else HBM if i in takes else VMEM for i, operand in enumerate(operands)
        ],
        out_specs=[HBM if i in gives else VMEM for i in range(len(shapes))],
        scratch_shapes=list(scratch),
        compiler_params=pltpu.CompilerParams(vmem_limit_bytes=limit * 2**20),
        cost_estimate=pl.CostEstimate(flops=flops, bytes_accessed=4 * 2**20, transcendentals=0),
        name=name,
    )(*operands)


def body(momentum, gradient, right_basis):
    cols, width = right_basis.shape
    rows = momentum.shape[0]
    rank = width * lax.axis_size("row")
    members, uppers = chips("wide")[2], chips("long")[2]
    core = (lax.axis_index("col") % CORES).astype(jnp.int32).reshape(1)
    with jax.named_scope("basis_gather"):
        basis = gather(gather(right_basis.T, "long"), "wide").reshape(rank, cols)
    blended = momentum + gradient.astype(jnp.float32)
    with jax.named_scope("left"):
        left_own, left_other = halves(dot(basis, blended, (1, 1), HIGH))
        left_own = left_own + swap(left_other)
        left_own = gather(scatter_sum(left_own.reshape(Y, -1, rows), "y"), "y").reshape(-1, rows)
        left = join(left_own, swap(left_own)).reshape(X, 2, uppers, width, rows)
        left = left.transpose(0, 2, 1, 3, 4).reshape(rank, rows)
    with jax.named_scope("sums"):
        tiles = width // 8 * (cols // BLOCK)
        per_core = (len(CORE_BLOCKS[0]) + 1) // 2
        shape = (members, uppers, tiles + per_core, 8, BLOCK)
        (sums,) = call(products_kernel, "products", [shape], 2 * 10**9, core, left, blended)
        sums = gather(scatter_sum(scatter_sum(sums, "wide"), "long"), "long")
        gram_own = gather(sums[:, tiles:], "wide")
        (raw,) = call(copies_kernel, "copies", [(members, rank // members, cols)], 10**6, sums)
        gram_own, raw = lax.optimization_barrier((gram_own, raw))
        gram_other = swap(gram_own)
        right_raw = exchange(raw, "wide").reshape(rank, cols)
    with jax.named_scope("factor"):
        (inverse,) = call(
            factor_kernel,
            "inverse_factor",
            [(rank, rank)],
            2 * 10**9,
            core,
            gram_own,
            gram_other,
            scratch=[
                pltpu.VMEM(gram_own.shape, jnp.float32),
                pltpu.VMEM(gram_own.shape, jnp.float32),
                pltpu.VMEM((rank, rank), jnp.float32),
                pltpu.VMEM((rank, rank), jnp.float32),
                pltpu.SemaphoreType.DMA((3,)),
            ],
            takes=(1, 2),
            gives=(0,),
        )
    with jax.named_scope("right"):
        shapes = [(rank, cols), (rank, rows), (rank // BLOCK, BLOCK)]
        scratch = [pltpu.VMEM((rank, width), jnp.float32) for width in (rank, cols, rows)]
        scratch += [pltpu.SemaphoreType.DMA((rank // BLOCK,)), pltpu.SemaphoreType.DMA((2, rank // BLOCK))]
        right, ortho, squares = call(
            right_kernel,
            "right",
            shapes,
            2 * 10**9,
            inverse,
            right_raw,
            left,
            scratch=scratch,
            limit=14,
            takes=(0,),
            gives=(0, 1),
        )
    with jax.named_scope("squares"):
        squares = jnp.broadcast_to(squares[None], (lax.axis_size("col"),) + squares.shape)
        squares = lax.all_to_all(squares, "col", 0, 0, tiled=False)
    with jax.named_scope("outputs"):
        (new_momentum,) = call(momentum_kernel, "momentum", [(rows, cols)], 10**9, blended, ortho, right)
        start = (lax.axis_index("row") * width).astype(jnp.int32).reshape(1)
        shapes = [(rows, cols), (width, cols)]
        scratch = [pltpu.VMEM((rank, BLOCK), jnp.float32)]
        update, new_basis = call(
            update_kernel, "update", shapes, 10**9, start, squares, ortho, right, scratch=scratch
        )
        new_basis = new_basis.T
    return (update, new_momentum, new_basis)


def solution(mesh):
    in_specs = (P("row", "col"), P("row", "col"), P("col", "row"))
    out_specs = (P("row", "col"), P("row", "col"), P("col", "row"))
    return jax.shard_map(body, mesh=mesh, in_specs=in_specs, out_specs=out_specs, check_vma=False)
```

```python
import math

import jax
import jax.numpy as jnp
from jax import lax
from jax.experimental import pallas as pl
from jax.experimental.pallas import tpu as pltpu
from jax.sharding import PartitionSpec as P

ROWS = 8192
COLS = 14336
RANK = 512
BLOCK = 128
X, Y, Z, CORES = 4, 8, 8, 2
CORE_BLOCKS = (
    ((0, 0), (0, 1), (0, 2), (0, 3), (1, 1)),
    ((1, 2), (1, 3), (2, 2), (2, 3), (3, 3)),
)


HIGH = lax.Precision.HIGH
HIGHEST = lax.Precision.HIGHEST
epsilon_norm = 1e-06
retain = 0.7


def dot(first, second, over, precision):
    return lax.dot_general(
        first, second, ((over[:1], over[1:]), ((), ())), precision=precision, preferred_element_type=jnp.float32
    )


def chips(way):
    upper = Z // 2
    row = lambda x, high, low: (x * upper + high) * 2 + low
    if way == "wide":
        return "row", [[row(x, high, low) for x in range(X) for low in range(2)] for high in range(upper)], 2 * X
    if way == "long":
        return "row", [[row(x, high, low) for high in range(upper)] for x in range(X) for low in range(2)], upper
    return "col", [[y * CORES + core for y in range(Y)] for core in range(CORES)], Y


def exchange(blocks, way):
    name, groups, _ = chips(way)
    return lax.all_to_all(blocks, name, 0, 0, axis_index_groups=groups, tiled=False)


def scatter_sum(blocks, way):
    return jnp.sum(exchange(blocks, way), axis=0)


def copies(part, way):
    return jnp.broadcast_to(part[None], (chips(way)[2],) + part.shape)


def gather(part, way):
    return exchange(copies(part, way), way)


def swap(part):
    return lax.ppermute(part, "col", [(i, i ^ 1) for i in range(Y * CORES)])


def halves(whole):
    half = whole.shape[0] // CORES
    core = lax.axis_index("col") % CORES
    return (
        lax.dynamic_slice_in_dim(whole, core * half, half, 0),
        lax.dynamic_slice_in_dim(whole, (1 - core) * half, half, 0),
    )


def join(own, other):
    first = lax.axis_index("col") % CORES == 0
    return jnp.concatenate([jnp.where(first, own, other), jnp.where(first, other, own)], axis=0)


def split(value):
    high = value.astype(jnp.bfloat16)
    return high, (value - high.astype(jnp.float32)).astype(jnp.bfloat16)


def dot3(first, second, over):
    one = lambda a, b: lax.dot_general(
        a, b, ((over[:1], over[1:]), ((), ())), preferred_element_type=jnp.float32
    )
    return one(first[0], second[0]) + (one(first[0], second[1]) + one(first[1], second[0]))


def square(k):
    return pl.ds(k * BLOCK, BLOCK)


def products_kernel(core_ref, left_ref, blended_ref, out_ref):
    members, uppers = out_ref.shape[:2]
    deep = left_ref.shape[0] // (8 * members * uppers)
    lanes = blended_ref.shape[1] // BLOCK
    right = dot3(split(left_ref[...]), split(blended_ref[...]), (1, 0))
    for j in range(lanes):
        tiles = right[:, j * BLOCK : (j + 1) * BLOCK].reshape(members, uppers, deep, 8, BLOCK)
        for i in range(deep):
            out_ref[:, :, i * lanes + j] = tiles[:, :, i]

    def gram(blocks):
        found = [dot(left_ref[square(k), :], left_ref[square(l), :], (1, 1), HIGHEST) for k, l in blocks]
        found.append(jnp.zeros((BLOCK, BLOCK), jnp.float32))
        for t in range(len(found) // 2):
            pair = jnp.concatenate(found[2 * t : 2 * t + 2], axis=0)
            out_ref[:, :, deep * lanes + t] = pair.reshape(members, uppers, 8, BLOCK)

    pl.when(core_ref[0] == 0)(lambda: gram(CORE_BLOCKS[0]))
    pl.when(core_ref[0] != 0)(lambda: gram(CORE_BLOCKS[1]))


def copies_kernel(sums_ref, out_ref):
    members, rows, cols = out_ref.shape
    uppers = sums_ref.shape[0]
    deep, lanes = rows // (8 * uppers), cols // BLOCK
    for j in range(lanes):
        tiles = [sums_ref[:, i * lanes + j] for i in range(deep)]
        piece = jnp.stack(tiles, axis=1).reshape(rows, BLOCK)
        for member in range(members):
            out_ref[member, :, j * BLOCK : (j + 1) * BLOCK] = piece


def invert_block(block):
    groups = BLOCK // 8
    sub = lax.broadcasted_iota(jnp.int32, (8, BLOCK), 0)
    lane = lax.broadcasted_iota(jnp.int32, (8, BLOCK), 1)
    work = [block[8 * q : 8 * q + 8, :] for q in range(groups)]
    side = [jnp.where(lane == sub + 8 * q, 1.0, 0.0).astype(jnp.float32) for q in range(groups)]
    out = []
    for p in range(groups):
        spread = {
            q: [jnp.broadcast_to(work[q][:, 8 * p + j : 8 * p + j + 1], (8, BLOCK)) for j in range(8)]
            for q in range(p, groups)
        }
        pivots = jnp.ones((8, BLOCK), jnp.float32)
        for j in range(8):
            row = [jnp.broadcast_to(spread[p][k][j : j + 1, :], (8, BLOCK)) for k in range(j, 8)]
            pivots = jnp.where(sub == j, row[0], pivots)
            inverse = 1.0 / row[0]
            row_work = jnp.broadcast_to(work[p][j : j + 1, :], (8, BLOCK))
            row_side = jnp.broadcast_to(side[p][j : j + 1, :], (8, BLOCK))
            for q in range(p, groups):
                times = spread[q][j] * inverse
                if q == p:
                    times = jnp.where(sub > j, times, 0.0)
                for k in range(j + 1, 8):
                    spread[q][k] = spread[q][k] - times * row[k - j]
                work[q] = work[q] - times * row_work
                side[q] = side[q] - times * row_side
        out.append(side[p] * lax.rsqrt(pivots))
    return jnp.concatenate(out, axis=0)


def factor_kernel(core_ref, own_hbm, other_hbm, out_hbm, own_ref, other_ref, out_ref, work, sems):
    rank = out_ref.shape[0]
    count = rank // BLOCK
    arrive = [
        pltpu.make_async_copy(own_hbm, own_ref, sems.at[0]),
        pltpu.make_async_copy(other_hbm, other_ref, sems.at[1]),
    ]
    for part in arrive:
        part.start()
    work[...] = jnp.zeros((rank, rank), jnp.float32)

    def place(parts):
        for part_ref, blocks in zip(parts, CORE_BLOCKS):
            half = part_ref.shape[0] // 2
            for i, (k, l) in enumerate(blocks):
                tiles = part_ref[i % 2 * half : (i % 2 + 1) * half, :, i // 2]
                work[square(k), square(l)] = tiles.reshape(BLOCK, BLOCK)

    for part in arrive:
        part.wait()
    pl.when(core_ref[0] == 0)(lambda: place((own_ref, other_ref)))
    pl.when(core_ref[0] != 0)(lambda: place((other_ref, own_ref)))
    rows = lax.broadcasted_iota(jnp.int32, (rank, rank), 0)
    cols = lax.broadcasted_iota(jnp.int32, (rank, rank), 1)
    out_ref[...] = jnp.where(rows == cols, 1.0, 0.0)

    def step(k, carry):
        at = pl.ds(pl.multiple_of(k * BLOCK, BLOCK), BLOCK)
        inverse = invert_block(work[at, at])
        upper = dot(inverse, work[at, :], (1, 0), HIGHEST)
        side = dot(inverse, out_ref[at, :], (1, 0), HIGHEST)
        out_ref[at, :] = side
        for i in range(1, count):

            @pl.when(i > k)
            def _():
                below = pl.ds(i * BLOCK, BLOCK)
                times = upper[:, i * BLOCK : (i + 1) * BLOCK]
                work[below, :] -= dot(times, upper, (0, 0), HIGHEST)
                out_ref[below, :] -= dot(times, side, (0, 0), HIGHEST)

        return carry

    lax.fori_loop(0, count, step, 0)
    leave = pltpu.make_async_copy(out_ref, out_hbm, sems.at[2])
    leave.start()
    leave.wait()


def right_kernel(
    inverse_hbm, raw_ref, left_ref, right_hbm, ortho_hbm, squares_ref, inverse_ref, right_ref, ortho_ref, arrive, leave
):
    count = raw_ref.shape[0] // BLOCK
    blocks = [pltpu.make_async_copy(inverse_hbm.at[square(i)], inverse_ref.at[square(i)], arrive.at[i]) for i in range(count)]
    for block in blocks:
        block.start()
    raw, left = split(raw_ref[...]), split(left_ref[...])
    eye = lax.broadcasted_iota(jnp.int32, (BLOCK, BLOCK), 0) == lax.broadcasted_iota(jnp.int32, (BLOCK, BLOCK), 1)
    out = []
    for i in range(count):
        at, upto = square(i), (i + 1) * BLOCK
        blocks[i].wait()
        inverse = split(inverse_ref[at, :upto])
        right = dot3(inverse, [part[:upto] for part in raw], (1, 0))
        right_ref[at, :] = right
        ortho_ref[at, :] = dot3(inverse, [part[:upto] for part in left], (1, 0))
        out.append(pltpu.make_async_copy(right_ref.at[at], right_hbm.at[at], leave.at[0, i]))
        out.append(pltpu.make_async_copy(ortho_ref.at[at], ortho_hbm.at[at], leave.at[1, i]))
        out[-2].start()
        out[-1].start()
        sums = jnp.sum(right * right, axis=1, keepdims=True)
        squares_ref[pl.ds(i, 1), :] = jnp.sum(jnp.where(eye, sums, 0.0), axis=0, keepdims=True)
    for block in out:
        block.wait()


def momentum_kernel(blended_ref, ortho_ref, right_ref, out_ref):
    out_ref[...] = blended_ref[...] - (1.0 - retain) * dot3(split(ortho_ref[...]), split(right_ref[...]), (0, 0))


def update_kernel(start_ref, squares_ref, ortho_ref, right_ref, update_ref, basis_ref, scaled):
    scale = math.sqrt(ROWS * COLS / RANK)
    rank, width = ortho_ref.shape[0], basis_ref.shape[0]
    rows = jnp.sum(squares_ref[...], axis=0)
    factors = lax.rsqrt(rows + epsilon_norm)
    eye = lax.broadcasted_iota(jnp.int32, (BLOCK, BLOCK), 0) == lax.broadcasted_iota(jnp.int32, (BLOCK, BLOCK), 1)
    for i in range(rank // BLOCK):
        at = pl.ds(i * BLOCK, BLOCK)
        column = jnp.sum(jnp.where(eye, factors[i : i + 1, :], 0.0), axis=1, keepdims=True)
        scaled[at, :] = jnp.broadcast_to(column, (BLOCK, BLOCK))
    ortho = ortho_ref[...] * (scale * scaled[:, :1])
    update_ref[...] = dot3(split(ortho), split(right_ref[...]), (0, 0))
    own = pl.ds(pl.multiple_of(start_ref[0], width), width)
    basis_ref[...] = right_ref[own, :] * scaled[own, :1]


VMEM = pl.BlockSpec(memory_space=pltpu.VMEM)
SMEM = pl.BlockSpec(memory_space=pltpu.SMEM)
HBM = pl.BlockSpec(memory_space=pltpu.HBM)


def call(kernel, name, shapes, flops, *operands, scratch=(), limit=10, takes=(), gives=()):
    return pl.pallas_call(
        kernel,
        out_shape=[
            pltpu.HBM(shape, jnp.float32) if i in gives else jax.ShapeDtypeStruct(shape, jnp.float32)
            for i, shape in enumerate(shapes)
        ],
        in_specs=[
            SMEM if operand.dtype == jnp.int32 else HBM if i in takes else VMEM for i, operand in enumerate(operands)
        ],
        out_specs=[HBM if i in gives else VMEM for i in range(len(shapes))],
        scratch_shapes=list(scratch),
        compiler_params=pltpu.CompilerParams(vmem_limit_bytes=limit * 2**20),
        cost_estimate=pl.CostEstimate(flops=flops, bytes_accessed=4 * 2**20, transcendentals=0),
        name=name,
    )(*[pltpu.with_memory_space_constraint(x, pltpu.HBM) if i in takes else x for i, x in enumerate(operands)])


def body(momentum, gradient, right_basis):
    cols, width = right_basis.shape
    rows = momentum.shape[0]
    rank = width * lax.axis_size("row")
    members, uppers = chips("wide")[2], chips("long")[2]
    core = (lax.axis_index("col") % CORES).astype(jnp.int32).reshape(1)
    with jax.named_scope("basis_gather"):
        basis = gather(gather(right_basis.T, "long"), "wide").reshape(rank, cols)
    blended = momentum + gradient.astype(jnp.float32)
    with jax.named_scope("left"):
        left_own, left_other = halves(dot(basis, blended, (1, 1), HIGH))
        left_own = left_own + swap(left_other)
        left_own = gather(scatter_sum(left_own.reshape(Y, -1, rows), "y"), "y").reshape(-1, rows)
        left = join(left_own, swap(left_own)).reshape(X, 2, uppers, width, rows)
        left = left.transpose(0, 2, 1, 3, 4).reshape(rank, rows)
    with jax.named_scope("sums"):
        tiles = width // 8 * (cols // BLOCK)
        per_core = (len(CORE_BLOCKS[0]) + 1) // 2
        shape = (members, uppers, tiles + per_core, 8, BLOCK)
        (sums,) = call(products_kernel, "products", [shape], 2 * 10**9, core, left, blended)
        sums = gather(scatter_sum(scatter_sum(sums, "wide"), "long"), "long")
        gram_own = gather(sums[:, tiles:], "wide")
        (raw,) = call(copies_kernel, "copies", [(members, rank // members, cols)], 10**6, sums)
        gram_own, raw = lax.optimization_barrier((gram_own, raw))
        gram_other = swap(gram_own)
        right_raw = exchange(raw, "wide").reshape(rank, cols)
    with jax.named_scope("factor"):
        (inverse,) = call(
            factor_kernel,
            "inverse_factor",
            [(rank, rank)],
            2 * 10**9,
            core,
            gram_own,
            gram_other,
            scratch=[
                pltpu.VMEM(gram_own.shape, jnp.float32),
                pltpu.VMEM(gram_own.shape, jnp.float32),
                pltpu.VMEM((rank, rank), jnp.float32),
                pltpu.VMEM((rank, rank), jnp.float32),
                pltpu.SemaphoreType.DMA((3,)),
            ],
            takes=(1, 2),
            gives=(0,),
        )
    with jax.named_scope("right"):
        shapes = [(rank, cols), (rank, rows), (rank // BLOCK, BLOCK)]
        scratch = [pltpu.VMEM((rank, width), jnp.float32) for width in (rank, cols, rows)]
        scratch += [pltpu.SemaphoreType.DMA((rank // BLOCK,)), pltpu.SemaphoreType.DMA((2, rank // BLOCK))]
        right, ortho, squares = call(
            right_kernel,
            "right",
            shapes,
            2 * 10**9,
            inverse,
            right_raw,
            left,
            scratch=scratch,
            limit=14,
            takes=(0,),
            gives=(0, 1),
        )
    with jax.named_scope("squares"):
        squares = jnp.broadcast_to(squares[None], (lax.axis_size("col"),) + squares.shape)
        squares = lax.all_to_all(squares, "col", 0, 0, tiled=False)
    with jax.named_scope("outputs"):
        (new_momentum,) = call(momentum_kernel, "momentum", [(rows, cols)], 10**9, blended, ortho, right)
        start = (lax.axis_index("row") * width).astype(jnp.int32).reshape(1)
        shapes = [(rows, cols), (width, cols)]
        scratch = [pltpu.VMEM((rank, BLOCK), jnp.float32)]
        update, new_basis = call(
            update_kernel, "update", shapes, 10**9, start, squares, ortho, right, scratch=scratch
        )
        new_basis = new_basis.T
    return (update, new_momentum, new_basis)


def solution(mesh):
    in_specs = (P("row", "col"), P("row", "col"), P("col", "row"))
    out_specs = (P("row", "col"), P("row", "col"), P("col", "row"))
    return jax.shard_map(body, mesh=mesh, in_specs=in_specs, out_specs=out_specs, check_vma=False)
```

```python
import functools
import math

import jax
import jax.numpy as jnp
from jax import lax
from jax.experimental import pallas as pl
from jax.experimental.pallas import tpu as pltpu
from jax.sharding import PartitionSpec as P

ROWS = 8192
COLS = 14336
RANK = 512
BLOCK = 128
X, Y, Z, CORES = 4, 8, 8, 2
CORE_BLOCKS = (
    ((0, 0), (0, 1), (0, 2), (0, 3), (1, 1)),
    ((1, 2), (1, 3), (2, 2), (2, 3), (3, 3)),
)


HIGH = lax.Precision.HIGH
HIGHEST = lax.Precision.HIGHEST
epsilon_norm = 1e-06
retain = 0.7


def dot(first, second, over, precision):
    return lax.dot_general(
        first, second, ((over[:1], over[1:]), ((), ())), precision=precision, preferred_element_type=jnp.float32
    )


def chips(way):
    upper = Z // 2
    row = lambda x, high, low: (x * upper + high) * 2 + low
    if way == "wide":
        return "row", [[row(x, high, low) for x in range(X) for low in range(2)] for high in range(upper)], 2 * X
    if way == "long":
        return "row", [[row(x, high, low) for high in range(upper)] for x in range(X) for low in range(2)], upper
    return "col", [[y * CORES + core for y in range(Y)] for core in range(CORES)], Y


def exchange(blocks, way):
    name, groups, _ = chips(way)
    return lax.all_to_all(blocks, name, 0, 0, axis_index_groups=groups, tiled=False)


def scatter_sum(blocks, way):
    return jnp.sum(exchange(blocks, way), axis=0)


def copies(part, way):
    return jnp.broadcast_to(part[None], (chips(way)[2],) + part.shape)


def gather(part, way):
    return exchange(copies(part, way), way)


def swap(part):
    return lax.ppermute(part, "col", [(i, i ^ 1) for i in range(Y * CORES)])


def halves(whole):
    half = whole.shape[0] // CORES
    core = lax.axis_index("col") % CORES
    return (
        lax.dynamic_slice_in_dim(whole, core * half, half, 0),
        lax.dynamic_slice_in_dim(whole, (1 - core) * half, half, 0),
    )


def join(own, other):
    first = lax.axis_index("col") % CORES == 0
    return jnp.concatenate([jnp.where(first, own, other), jnp.where(first, other, own)], axis=0)


def split(value):
    high = value.astype(jnp.bfloat16)
    return high, (value - high.astype(jnp.float32)).astype(jnp.bfloat16)


def dot3(first, second, over):
    one = lambda a, b: lax.dot_general(
        a, b, ((over[:1], over[1:]), ((), ())), preferred_element_type=jnp.float32
    )
    return one(first[0], second[0]) + (one(first[0], second[1]) + one(first[1], second[0]))


def square(k):
    return pl.ds(k * BLOCK, BLOCK)


def products_kernel(core_ref, left_ref, blended_ref, out_ref):
    members, uppers = out_ref.shape[:2]
    deep = left_ref.shape[0] // (8 * members * uppers)
    lanes = blended_ref.shape[1] // BLOCK
    right = dot3(split(left_ref[...]), split(blended_ref[...]), (1, 0))
    for j in range(lanes):
        tiles = right[:, j * BLOCK : (j + 1) * BLOCK].reshape(members, uppers, deep, 8, BLOCK)
        for i in range(deep):
            out_ref[:, :, i * lanes + j] = tiles[:, :, i]

    def gram(blocks):
        found = [dot(left_ref[square(k), :], left_ref[square(l), :], (1, 1), HIGHEST) for k, l in blocks]
        found.append(jnp.zeros((BLOCK, BLOCK), jnp.float32))
        for t in range(len(found) // 2):
            pair = jnp.concatenate(found[2 * t : 2 * t + 2], axis=0)
            out_ref[:, :, deep * lanes + t] = pair.reshape(members, uppers, 8, BLOCK)

    pl.when(core_ref[0] == 0)(lambda: gram(CORE_BLOCKS[0]))
    pl.when(core_ref[0] != 0)(lambda: gram(CORE_BLOCKS[1]))


def copies_kernel(sums_ref, out_ref):
    members, rows, cols = out_ref.shape
    uppers = sums_ref.shape[0]
    deep, lanes = rows // (8 * uppers), cols // BLOCK
    for j in range(lanes):
        tiles = [sums_ref[:, i * lanes + j] for i in range(deep)]
        piece = jnp.stack(tiles, axis=1).reshape(rows, BLOCK)
        for member in range(members):
            out_ref[member, :, j * BLOCK : (j + 1) * BLOCK] = piece


def invert_block(block, pending):
    groups = BLOCK // 8
    sub = lax.broadcasted_iota(jnp.int32, (8, BLOCK), 0)
    lane = lax.broadcasted_iota(jnp.int32, (8, BLOCK), 1)
    work = [block[8 * q : 8 * q + 8, :] for q in range(groups)]
    side = [jnp.where(lane == sub + 8 * q, 1.0, 0.0).astype(jnp.float32) for q in range(groups)]
    out = []
    for p in range(groups):
        if pending:
            pending.pop(0)()
        spread = {
            q: [jnp.broadcast_to(work[q][:, 8 * p + j : 8 * p + j + 1], (8, BLOCK)) for j in range(8)]
            for q in range(p, groups)
        }
        pivots = jnp.ones((8, BLOCK), jnp.float32)
        for j in range(8):
            row = [jnp.broadcast_to(spread[p][k][j : j + 1, :], (8, BLOCK)) for k in range(j, 8)]
            pivots = jnp.where(sub == j, row[0], pivots)
            inverse = 1.0 / row[0]
            row_work = jnp.broadcast_to(work[p][j : j + 1, :], (8, BLOCK))
            row_side = jnp.broadcast_to(side[p][j : j + 1, :], (8, BLOCK))
            for q in range(p, groups):
                times = spread[q][j] * inverse
                if q == p:
                    times = jnp.where(sub > j, times, 0.0)
                for k in range(j + 1, 8):
                    spread[q][k] = spread[q][k] - times * row[k - j]
                work[q] = work[q] - times * row_work
                side[q] = side[q] - times * row_side
        out.append(side[p] * lax.rsqrt(pivots))
    return jnp.concatenate(out, axis=0)


def eliminate(work):
    count = work.shape[0] // BLOCK
    span = lambda first, last: pl.ds(first * BLOCK, (last - first) * BLOCK)
    pending = []
    for k in range(count):
        inverse = invert_block(work[square(k), square(k)], pending)
        while pending:
            pending.pop(0)()
        work[square(k), square(k)] = inverse
        if k + 1 < count:
            near = dot(inverse, work[square(k), square(k + 1)], (1, 0), HIGHEST)
            work[square(k), square(k + 1)] = near
            work[square(k + 1), square(k + 1)] -= dot(near, near, (0, 0), HIGHEST)

        def row(first, last, k=k, inverse=inverse):
            at = (square(k), span(first, last))
            work[at] = dot(inverse, work[at], (1, 0), HIGHEST)

        def below(i, first, last, k=k):
            change = dot(work[square(k), square(i)], work[square(k), span(first, last)], (0, 0), HIGHEST)
            at = (square(i), span(first, last))
            work[at] = -change if first == k else work[at] - change

        if k + 2 < count:
            pending.append(functools.partial(row, k + 2, count))
        if k:
            pending.append(functools.partial(row, 0, k))
        for i in range(k + 1, count):
            right = max(i, k + 2)
            if right < count:
                pending.append(functools.partial(below, i, right, count))
            pending.append(functools.partial(below, i, k, k + 1))
            if k:
                pending.append(functools.partial(below, i, 0, k))
    while pending:
        pending.pop(0)()


def factor_kernel(
    core_ref, own_hbm, other_hbm, left_ref, out_hbm, ortho_hbm, own_ref, other_ref, work, ortho_ref, sems
):
    rank = work.shape[0]
    arrive = [
        pltpu.make_async_copy(own_hbm, own_ref, sems.at[0]),
        pltpu.make_async_copy(other_hbm, other_ref, sems.at[1]),
    ]
    for part in arrive:
        part.start()

    def place(parts):
        for part_ref, blocks in zip(parts, CORE_BLOCKS):
            half = part_ref.shape[0] // 2
            for i, (k, l) in enumerate(blocks):
                tiles = part_ref[i % 2 * half : (i % 2 + 1) * half, :, i // 2]
                work[square(k), square(l)] = tiles.reshape(BLOCK, BLOCK)

    for part in arrive:
        part.wait()
    pl.when(core_ref[0] == 0)(lambda: place((own_ref, other_ref)))
    pl.when(core_ref[0] != 0)(lambda: place((other_ref, own_ref)))
    eliminate(work)
    leave = [pltpu.make_async_copy(work, out_hbm, sems.at[2]), pltpu.make_async_copy(ortho_ref, ortho_hbm, sems.at[3])]
    leave[0].start()
    left = split(left_ref[...])
    for i in range(rank // BLOCK):
        upto = (i + 1) * BLOCK
        ortho_ref[square(i), :] = dot3(split(work[square(i), :upto]), [part[:upto] for part in left], (1, 0))
    leave[1].start()
    for part in leave:
        part.wait()


def right_kernel(inverse_hbm, raw_ref, right_hbm, squares_ref, inverse_ref, right_ref, arrive, leave):
    count = raw_ref.shape[0] // BLOCK
    blocks = [
        pltpu.make_async_copy(inverse_hbm.at[square(i)], inverse_ref.at[square(i)], arrive.at[i]) for i in range(count)
    ]
    for block in blocks:
        block.start()
    raw = split(raw_ref[...])
    eye = lax.broadcasted_iota(jnp.int32, (BLOCK, BLOCK), 0) == lax.broadcasted_iota(jnp.int32, (BLOCK, BLOCK), 1)
    out = []
    for i in range(count):
        at, upto = square(i), (i + 1) * BLOCK
        blocks[i].wait()
        right = dot3(split(inverse_ref[at, :upto]), [part[:upto] for part in raw], (1, 0))
        right_ref[at, :] = right
        out.append(pltpu.make_async_copy(right_ref.at[at], right_hbm.at[at], leave.at[i]))
        out[-1].start()
        sums = jnp.sum(right * right, axis=1, keepdims=True)
        squares_ref[pl.ds(i, 1), :] = jnp.sum(jnp.where(eye, sums, 0.0), axis=0, keepdims=True)
    for block in out:
        block.wait()


def momentum_kernel(blended_ref, ortho_ref, right_ref, out_ref):
    out_ref[...] = blended_ref[...] - (1.0 - retain) * dot3(split(ortho_ref[...]), split(right_ref[...]), (0, 0))


def update_kernel(start_ref, squares_ref, ortho_ref, right_ref, update_ref, basis_ref, scaled):
    scale = math.sqrt(ROWS * COLS / RANK)
    rank, width = ortho_ref.shape[0], basis_ref.shape[0]
    rows = jnp.sum(squares_ref[...], axis=0)
    factors = lax.rsqrt(rows + epsilon_norm)
    eye = lax.broadcasted_iota(jnp.int32, (BLOCK, BLOCK), 0) == lax.broadcasted_iota(jnp.int32, (BLOCK, BLOCK), 1)
    for i in range(rank // BLOCK):
        at = pl.ds(i * BLOCK, BLOCK)
        column = jnp.sum(jnp.where(eye, factors[i : i + 1, :], 0.0), axis=1, keepdims=True)
        scaled[at, :] = jnp.broadcast_to(column, (BLOCK, BLOCK))
    ortho = ortho_ref[...] * (scale * scaled[:, :1])
    update_ref[...] = dot3(split(ortho), split(right_ref[...]), (0, 0))
    own = pl.ds(pl.multiple_of(start_ref[0], width), width)
    basis_ref[...] = right_ref[own, :] * scaled[own, :1]


VMEM = pl.BlockSpec(memory_space=pltpu.VMEM)
SMEM = pl.BlockSpec(memory_space=pltpu.SMEM)
HBM = pl.BlockSpec(memory_space=pltpu.HBM)


def call(kernel, name, shapes, flops, *operands, scratch=(), limit=10, takes=(), gives=()):
    return pl.pallas_call(
        kernel,
        out_shape=[
            pltpu.HBM(shape, jnp.float32) if i in gives else jax.ShapeDtypeStruct(shape, jnp.float32)
            for i, shape in enumerate(shapes)
        ],
        in_specs=[
            SMEM if operand.dtype == jnp.int32 else HBM if i in takes else VMEM for i, operand in enumerate(operands)
        ],
        out_specs=[HBM if i in gives else VMEM for i in range(len(shapes))],
        scratch_shapes=list(scratch),
        compiler_params=pltpu.CompilerParams(vmem_limit_bytes=limit * 2**20),
        cost_estimate=pl.CostEstimate(flops=flops, bytes_accessed=4 * 2**20, transcendentals=0),
        name=name,
    )(*[pltpu.with_memory_space_constraint(x, pltpu.HBM) if i in takes else x for i, x in enumerate(operands)])


def body(momentum, gradient, right_basis):
    cols, width = right_basis.shape
    rows = momentum.shape[0]
    rank = width * lax.axis_size("row")
    members, uppers = chips("wide")[2], chips("long")[2]
    core = (lax.axis_index("col") % CORES).astype(jnp.int32).reshape(1)
    with jax.named_scope("basis_gather"):
        basis = gather(gather(right_basis.T, "long"), "wide").reshape(rank, cols)
    blended = momentum + gradient.astype(jnp.float32)
    with jax.named_scope("left"):
        left_own, left_other = halves(dot(basis, blended, (1, 1), HIGH))
        left_own = left_own + swap(left_other)
        left_own = gather(scatter_sum(left_own.reshape(Y, -1, rows), "y"), "y").reshape(-1, rows)
        left = join(left_own, swap(left_own)).reshape(X, 2, uppers, width, rows)
        left = left.transpose(0, 2, 1, 3, 4).reshape(rank, rows)
    with jax.named_scope("sums"):
        tiles = width // 8 * (cols // BLOCK)
        per_core = (len(CORE_BLOCKS[0]) + 1) // 2
        shape = (members, uppers, tiles + per_core, 8, BLOCK)
        (sums,) = call(products_kernel, "products", [shape], 2 * 10**9, core, left, blended)
        sums = gather(scatter_sum(scatter_sum(sums, "wide"), "long"), "long")
        gram_own = gather(sums[:, tiles:], "wide")
        (raw,) = call(copies_kernel, "copies", [(members, rank // members, cols)], 10**6, sums)
        gram_own, raw = lax.optimization_barrier((gram_own, raw))
        gram_other = swap(gram_own)
        right_raw = exchange(raw, "wide").reshape(rank, cols)
    with jax.named_scope("factor"):
        inverse, ortho = call(
            factor_kernel,
            "factor",
            [(rank, rank), (rank, rows)],
            2 * 10**9,
            core,
            gram_own,
            gram_other,
            left,
            scratch=[
                pltpu.VMEM(gram_own.shape, jnp.float32),
                pltpu.VMEM(gram_own.shape, jnp.float32),
                pltpu.VMEM((rank, rank), jnp.float32),
                pltpu.VMEM((rank, rows), jnp.float32),
                pltpu.SemaphoreType.DMA((4,)),
            ],
            takes=(1, 2),
            gives=(0, 1),
        )
    with jax.named_scope("right"):
        right, squares = call(
            right_kernel,
            "right",
            [(rank, cols), (rank // BLOCK, BLOCK)],
            2 * 10**9,
            inverse,
            right_raw,
            scratch=[
                pltpu.VMEM((rank, rank), jnp.float32),
                pltpu.VMEM((rank, cols), jnp.float32),
                pltpu.SemaphoreType.DMA((rank // BLOCK,)),
                pltpu.SemaphoreType.DMA((rank // BLOCK,)),
            ],
            limit=14,
            takes=(0,),
            gives=(0,),
        )
    with jax.named_scope("squares"):
        squares = jnp.broadcast_to(squares[None], (lax.axis_size("col"),) + squares.shape)
        squares = lax.all_to_all(squares, "col", 0, 0, tiled=False)
    with jax.named_scope("outputs"):
        (new_momentum,) = call(momentum_kernel, "momentum", [(rows, cols)], 10**9, blended, ortho, right)
        start = (lax.axis_index("row") * width).astype(jnp.int32).reshape(1)
        shapes = [(rows, cols), (width, cols)]
        scratch = [pltpu.VMEM((rank, BLOCK), jnp.float32)]
        update, new_basis = call(
            update_kernel, "update", shapes, 10**9, start, squares, ortho, right, scratch=scratch
        )
        new_basis = new_basis.T
    return (update, new_momentum, new_basis)


def solution(mesh):
    in_specs = (P("row", "col"), P("row", "col"), P("col", "row"))
    out_specs = (P("row", "col"), P("row", "col"), P("col", "row"))
    return jax.shard_map(body, mesh=mesh, in_specs=in_specs, out_specs=out_specs, check_vma=False)
```

```python
import functools
import math

import jax
import jax.numpy as jnp
from jax import lax
from jax.experimental import pallas as pl
from jax.experimental.pallas import tpu as pltpu
from jax.sharding import PartitionSpec as P

ROWS = 8192
COLS = 14336
RANK = 512
BLOCK = 128
X, Y, Z, CORES = 4, 8, 8, 2
CORE_BLOCKS = (
    ((0, 0), (0, 1), (0, 2), (0, 3), (1, 1)),
    ((1, 2), (1, 3), (2, 2), (2, 3), (3, 3)),
)


HIGHEST = lax.Precision.HIGHEST
epsilon_norm = 1e-06
retain = 0.7


def dot(first, second, over, precision):
    return lax.dot_general(
        first, second, ((over[:1], over[1:]), ((), ())), precision=precision, preferred_element_type=jnp.float32
    )


def chips(way):
    upper = Z // 2
    row = lambda x, high, low: (x * upper + high) * 2 + low
    if way == "wide":
        return "row", [[row(x, high, low) for x in range(X) for low in range(2)] for high in range(upper)], 2 * X
    if way == "long":
        return "row", [[row(x, high, low) for high in range(upper)] for x in range(X) for low in range(2)], upper
    return "col", [[y * CORES + core for y in range(Y)] for core in range(CORES)], Y


def exchange(blocks, way):
    name, groups, _ = chips(way)
    return lax.all_to_all(blocks, name, 0, 0, axis_index_groups=groups, tiled=False)


def copies(part, way):
    return jnp.broadcast_to(part[None], (chips(way)[2],) + part.shape)


def gather(part, way):
    return exchange(copies(part, way), way)


def swap(part):
    return lax.ppermute(part, "col", [(i, i ^ 1) for i in range(Y * CORES)])


def join(own, other):
    first = lax.axis_index("col") % CORES == 0
    return jnp.concatenate([jnp.where(first, own, other), jnp.where(first, other, own)], axis=0)


def split(value):
    high = value.astype(jnp.bfloat16)
    return high, (value - high.astype(jnp.float32)).astype(jnp.bfloat16)


def dot3(first, second, over):
    one = lambda a, b: lax.dot_general(
        a, b, ((over[:1], over[1:]), ((), ())), preferred_element_type=jnp.float32
    )
    return one(first[0], second[0]) + (one(first[0], second[1]) + one(first[1], second[0]))


def left_kernel(half_ref, basis_ref, blended_ref, out_ref):
    half = out_ref.shape[0]
    rows = pl.ds(pl.multiple_of(half_ref[0] * half, half), half)
    out_ref[...] = dot3(split(basis_ref[rows, :]), split(blended_ref[...]), (1, 1))


def sum_kernel(blocks_ref, out_ref):
    for i in range(out_ref.shape[0]):
        out_ref[i] = sum(blocks_ref[member, i] for member in range(blocks_ref.shape[0]))


def sum_copies_kernel(blocks_ref, out_ref):
    members = range(blocks_ref.shape[0])
    total = sum(blocks_ref[member] for member in members)
    for member in members:
        out_ref[member] = total


def square(k):
    return pl.ds(k * BLOCK, BLOCK)


def products_kernel(core_ref, left_ref, blended_ref, out_ref):
    members, uppers = out_ref.shape[:2]
    deep = left_ref.shape[0] // (8 * members * uppers)
    lanes = blended_ref.shape[1] // BLOCK
    right = dot3(split(left_ref[...]), split(blended_ref[...]), (1, 0))
    for j in range(lanes):
        tiles = right[:, j * BLOCK : (j + 1) * BLOCK].reshape(members, uppers, deep, 8, BLOCK)
        for i in range(deep):
            out_ref[:, :, i * lanes + j] = tiles[:, :, i]

    def gram(blocks):
        found = [dot(left_ref[square(k), :], left_ref[square(l), :], (1, 1), HIGHEST) for k, l in blocks]
        found.append(jnp.zeros((BLOCK, BLOCK), jnp.float32))
        for t in range(len(found) // 2):
            pair = jnp.concatenate(found[2 * t : 2 * t + 2], axis=0)
            out_ref[:, :, deep * lanes + t] = pair.reshape(members, uppers, 8, BLOCK)

    pl.when(core_ref[0] == 0)(lambda: gram(CORE_BLOCKS[0]))
    pl.when(core_ref[0] != 0)(lambda: gram(CORE_BLOCKS[1]))


def copies_kernel(sums_ref, out_ref):
    members, rows, cols = out_ref.shape
    uppers = sums_ref.shape[0]
    deep, lanes = rows // (8 * uppers), cols // BLOCK
    for j in range(lanes):
        tiles = [sums_ref[:, i * lanes + j] for i in range(deep)]
        piece = jnp.stack(tiles, axis=1).reshape(rows, BLOCK)
        for member in range(members):
            out_ref[member, :, j * BLOCK : (j + 1) * BLOCK] = piece


def invert_block(block, pending):
    groups = BLOCK // 8
    sub = lax.broadcasted_iota(jnp.int32, (8, BLOCK), 0)
    lane = lax.broadcasted_iota(jnp.int32, (8, BLOCK), 1)
    work = [block[8 * q : 8 * q + 8, :] for q in range(groups)]
    side = [jnp.where(lane == sub + 8 * q, 1.0, 0.0).astype(jnp.float32) for q in range(groups)]
    out = []
    for p in range(groups):
        if pending:
            pending.pop(0)()
        spread = {
            q: [jnp.broadcast_to(work[q][:, 8 * p + j : 8 * p + j + 1], (8, BLOCK)) for j in range(8)]
            for q in range(p, groups)
        }
        pivots = jnp.ones((8, BLOCK), jnp.float32)
        for j in range(8):
            row = [jnp.broadcast_to(spread[p][k][j : j + 1, :], (8, BLOCK)) for k in range(j, 8)]
            pivots = jnp.where(sub == j, row[0], pivots)
            inverse = 1.0 / row[0]
            row_work = jnp.broadcast_to(work[p][j : j + 1, :], (8, BLOCK))
            row_side = jnp.broadcast_to(side[p][j : j + 1, :], (8, BLOCK))
            for q in range(p, groups):
                times = spread[q][j] * inverse
                if q == p:
                    times = jnp.where(sub > j, times, 0.0)
                for k in range(j + 1, 8):
                    spread[q][k] = spread[q][k] - times * row[k - j]
                work[q] = work[q] - times * row_work
                side[q] = side[q] - times * row_side
        out.append(side[p] * lax.rsqrt(pivots))
    return jnp.concatenate(out, axis=0)


def eliminate(work, finish):
    count = work.shape[0] // BLOCK
    span = lambda first, last: pl.ds(first * BLOCK, (last - first) * BLOCK)
    pending = []
    for k in range(count):
        inverse = invert_block(work[square(k), square(k)], pending)
        while pending:
            pending.pop(0)()
        work[square(k), square(k)] = inverse
        if k + 1 < count:
            near = dot(inverse, work[square(k), square(k + 1)], (1, 0), HIGHEST)
            work[square(k), square(k + 1)] = near
            work[square(k + 1), square(k + 1)] -= dot(near, near, (0, 0), HIGHEST)

        def row(first, last, k=k, inverse=inverse):
            at = (square(k), span(first, last))
            work[at] = dot(inverse, work[at], (1, 0), HIGHEST)

        def below(i, first, last, k=k):
            change = dot(work[square(k), square(i)], work[square(k), span(first, last)], (0, 0), HIGHEST)
            at = (square(i), span(first, last))
            work[at] = -change if first == k else work[at] - change

        if k + 2 < count:
            pending.append(functools.partial(row, k + 2, count))
        if k:
            pending.append(functools.partial(row, 0, k))
        pending.append(functools.partial(finish, k))
        for i in range(k + 1, count):
            right = max(i, k + 2)
            if right < count:
                pending.append(functools.partial(below, i, right, count))
            pending.append(functools.partial(below, i, k, k + 1))
            if k:
                pending.append(functools.partial(below, i, 0, k))
    while pending:
        pending.pop(0)()


def factor_kernel(
    core_ref, own_hbm, other_hbm, left_ref, out_hbm, ortho_hbm, own_ref, other_ref, work, ortho_ref, high, low, sems
):
    arrive = [
        pltpu.make_async_copy(own_hbm, own_ref, sems.at[0]),
        pltpu.make_async_copy(other_hbm, other_ref, sems.at[1]),
    ]
    for part in arrive:
        part.start()
    high[...], low[...] = split(left_ref[...])

    def place(parts):
        for part_ref, blocks in zip(parts, CORE_BLOCKS):
            half = part_ref.shape[0] // 2
            for i, (k, l) in enumerate(blocks):
                tiles = part_ref[i % 2 * half : (i % 2 + 1) * half, :, i // 2]
                work[square(k), square(l)] = tiles.reshape(BLOCK, BLOCK)

    for part in arrive:
        part.wait()
    pl.when(core_ref[0] == 0)(lambda: place((own_ref, other_ref)))
    pl.when(core_ref[0] != 0)(lambda: place((other_ref, own_ref)))
    leave = []

    def finish(k):
        at, upto = square(k), pl.ds(0, (k + 1) * BLOCK)
        leave.append(pltpu.make_async_copy(work.at[at, upto], out_hbm.at[at, upto], sems.at[2 + 2 * k]))
        leave[-1].start()
        ortho_ref[at, :] = dot3(split(work[at, upto]), (high[upto, :], low[upto, :]), (1, 0))
        leave.append(pltpu.make_async_copy(ortho_ref.at[at], ortho_hbm.at[at], sems.at[3 + 2 * k]))
        leave[-1].start()

    eliminate(work, finish)
    for part in leave:
        part.wait()


def right_kernel(inverse_hbm, raw_ref, right_hbm, squares_ref, inverse_ref, right_ref, arrive, leave):
    count = raw_ref.shape[0] // BLOCK
    lower = [(square(i), pl.ds(0, (i + 1) * BLOCK)) for i in range(count)]
    blocks = [
        pltpu.make_async_copy(inverse_hbm.at[at], inverse_ref.at[at], arrive.at[i]) for i, at in enumerate(lower)
    ]
    for block in blocks:
        block.start()
    raw = split(raw_ref[...])
    eye = lax.broadcasted_iota(jnp.int32, (BLOCK, BLOCK), 0) == lax.broadcasted_iota(jnp.int32, (BLOCK, BLOCK), 1)
    out = []
    for i in range(count):
        at, upto = square(i), (i + 1) * BLOCK
        blocks[i].wait()
        right = dot3(split(inverse_ref[at, :upto]), [part[:upto] for part in raw], (1, 0))
        right_ref[at, :] = right
        out.append(pltpu.make_async_copy(right_ref.at[at], right_hbm.at[at], leave.at[i]))
        out[-1].start()
        sums = jnp.sum(right * right, axis=1, keepdims=True)
        squares_ref[pl.ds(i, 1), :] = jnp.sum(jnp.where(eye, sums, 0.0), axis=0, keepdims=True)
    for block in out:
        block.wait()


def momentum_kernel(blended_ref, ortho_ref, right_ref, out_ref):
    out_ref[...] = blended_ref[...] - (1.0 - retain) * dot3(split(ortho_ref[...]), split(right_ref[...]), (0, 0))


def update_kernel(start_ref, squares_ref, ortho_ref, right_ref, update_ref, basis_ref, scaled):
    scale = math.sqrt(ROWS * COLS / RANK)
    rank, width = ortho_ref.shape[0], basis_ref.shape[0]
    rows = jnp.sum(squares_ref[...], axis=0)
    factors = lax.rsqrt(rows + epsilon_norm)
    eye = lax.broadcasted_iota(jnp.int32, (BLOCK, BLOCK), 0) == lax.broadcasted_iota(jnp.int32, (BLOCK, BLOCK), 1)
    for i in range(rank // BLOCK):
        at = pl.ds(i * BLOCK, BLOCK)
        column = jnp.sum(jnp.where(eye, factors[i : i + 1, :], 0.0), axis=1, keepdims=True)
        scaled[at, :] = jnp.broadcast_to(column, (BLOCK, BLOCK))
    ortho = ortho_ref[...] * (scale * scaled[:, :1])
    update_ref[...] = dot3(split(ortho), split(right_ref[...]), (0, 0))
    own = pl.ds(pl.multiple_of(start_ref[0], width), width)
    basis_ref[...] = right_ref[own, :] * scaled[own, :1]


VMEM = pl.BlockSpec(memory_space=pltpu.VMEM)
SMEM = pl.BlockSpec(memory_space=pltpu.SMEM)
HBM = pl.BlockSpec(memory_space=pltpu.HBM)


def call(kernel, name, shapes, flops, *operands, scratch=(), limit=10, takes=(), gives=()):
    return pl.pallas_call(
        kernel,
        out_shape=[
            pltpu.HBM(shape, jnp.float32) if i in gives else jax.ShapeDtypeStruct(shape, jnp.float32)
            for i, shape in enumerate(shapes)
        ],
        in_specs=[
            SMEM if operand.dtype == jnp.int32 else HBM if i in takes else VMEM for i, operand in enumerate(operands)
        ],
        out_specs=[HBM if i in gives else VMEM for i in range(len(shapes))],
        scratch_shapes=list(scratch),
        compiler_params=pltpu.CompilerParams(vmem_limit_bytes=limit * 2**20),
        cost_estimate=pl.CostEstimate(flops=flops, bytes_accessed=4 * 2**20, transcendentals=0),
        name=name,
    )(*[pltpu.with_memory_space_constraint(x, pltpu.HBM) if i in takes else x for i, x in enumerate(operands)])


def body(momentum, gradient, right_basis):
    cols, width = right_basis.shape
    rows = momentum.shape[0]
    rank = width * lax.axis_size("row")
    members, uppers = chips("wide")[2], chips("long")[2]
    core = (lax.axis_index("col") % CORES).astype(jnp.int32).reshape(1)
    with jax.named_scope("basis_gather"):
        basis = gather(gather(right_basis.T, "long"), "wide").reshape(rank, cols)
    blended = momentum + gradient.astype(jnp.float32)
    with jax.named_scope("left"):
        half = [(rank // CORES, rows)]
        (left_other,) = call(left_kernel, "left_other", half, 10**9, 1 - core, basis, blended)
        left_other = swap(left_other)
        (left_own,) = call(left_kernel, "left_own", half, 10**9, core, basis, blended)
        parts = exchange((left_own + left_other).reshape(Y, -1, rows), "y")
        (parts,) = call(sum_copies_kernel, "left_sum", [parts.shape], 10**6, parts)
        left_own = exchange(parts, "y").reshape(-1, rows)
        left = join(left_own, swap(left_own)).reshape(X, 2, uppers, width, rows)
        left = left.transpose(0, 2, 1, 3, 4).reshape(rank, rows)
    with jax.named_scope("sums"):
        tiles = width // 8 * (cols // BLOCK)
        per_core = (len(CORE_BLOCKS[0]) + 1) // 2
        shape = (members, uppers, tiles + per_core, 8, BLOCK)
        (sums,) = call(products_kernel, "products", [shape], 2 * 10**9, core, left, blended)
        sums = exchange(sums, "wide")
        (sums,) = call(sum_kernel, "wide_sum", [sums.shape[1:]], 10**6, sums)
        sums = exchange(sums, "long")
        (sums,) = call(sum_copies_kernel, "long_sum", [sums.shape], 10**6, sums)
        sums = exchange(sums, "long")
        gram_own = gather(sums[:, tiles:], "wide")
        (raw,) = call(copies_kernel, "copies", [(members, rank // members, cols)], 10**6, sums)
        gram_own, raw = lax.optimization_barrier((gram_own, raw))
        gram_other = swap(gram_own)
        right_raw = exchange(raw, "wide").reshape(rank, cols)
    with jax.named_scope("factor"):
        inverse, ortho = call(
            factor_kernel,
            "factor",
            [(rank, rank), (rank, rows)],
            2 * 10**9,
            core,
            gram_own,
            gram_other,
            left,
            scratch=[
                pltpu.VMEM(gram_own.shape, jnp.float32),
                pltpu.VMEM(gram_own.shape, jnp.float32),
                pltpu.VMEM((rank, rank), jnp.float32),
                pltpu.VMEM((rank, rows), jnp.float32),
                pltpu.VMEM((rank, rows), jnp.bfloat16),
                pltpu.VMEM((rank, rows), jnp.bfloat16),
                pltpu.SemaphoreType.DMA((2 + 2 * (rank // BLOCK),)),
            ],
            takes=(1, 2),
            gives=(0, 1),
        )
    with jax.named_scope("right"):
        right, squares = call(
            right_kernel,
            "right",
            [(rank, cols), (rank // BLOCK, BLOCK)],
            2 * 10**9,
            inverse,
            right_raw,
            scratch=[
                pltpu.VMEM((rank, rank), jnp.float32),
                pltpu.VMEM((rank, cols), jnp.float32),
                pltpu.SemaphoreType.DMA((rank // BLOCK,)),
                pltpu.SemaphoreType.DMA((rank // BLOCK,)),
            ],
            limit=14,
            takes=(0,),
            gives=(0,),
        )
    with jax.named_scope("squares"):
        squares = jnp.broadcast_to(squares[None], (lax.axis_size("col"),) + squares.shape)
        squares = lax.all_to_all(squares, "col", 0, 0, tiled=False)
    with jax.named_scope("outputs"):
        (new_momentum,) = call(momentum_kernel, "momentum", [(rows, cols)], 10**9, blended, ortho, right)
        start = (lax.axis_index("row") * width).astype(jnp.int32).reshape(1)
        shapes = [(rows, cols), (width, cols)]
        scratch = [pltpu.VMEM((rank, BLOCK), jnp.float32)]
        update, new_basis = call(
            update_kernel, "update", shapes, 10**9, start, squares, ortho, right, scratch=scratch
        )
        new_basis = new_basis.T
    return (update, new_momentum, new_basis)


def solution(mesh):
    in_specs = (P("row", "col"), P("row", "col"), P("col", "row"))
    out_specs = (P("row", "col"), P("row", "col"), P("col", "row"))
    return jax.shard_map(body, mesh=mesh, in_specs=in_specs, out_specs=out_specs, check_vma=False)
```

```python
import functools
import math

import jax
import jax.numpy as jnp
from jax import lax
from jax.experimental import pallas as pl
from jax.experimental.pallas import tpu as pltpu
from jax.sharding import PartitionSpec as P

ROWS = 8192
COLS = 14336
RANK = 512
BLOCK = 128
X, Y, Z, CORES = 4, 8, 8, 2
CORE_BLOCKS = (
    ((0, 0), (0, 1), (0, 2), (0, 3), (1, 1)),
    ((1, 2), (1, 3), (2, 2), (2, 3), (3, 3)),
)


HIGHEST = lax.Precision.HIGHEST
epsilon_norm = 1e-06
retain = 0.7


def dot(first, second, over, precision):
    return lax.dot_general(
        first, second, ((over[:1], over[1:]), ((), ())), precision=precision, preferred_element_type=jnp.float32
    )


def chips(way):
    upper = Z // 2
    row = lambda x, high, low: (x * upper + high) * 2 + low
    if way == "wide":
        return "row", [[row(x, high, low) for x in range(X) for low in range(2)] for high in range(upper)], 2 * X
    if way == "long":
        return "row", [[row(x, high, low) for high in range(upper)] for x in range(X) for low in range(2)], upper
    return "col", [[y * CORES + core for y in range(Y)] for core in range(CORES)], Y


def exchange(blocks, way):
    name, groups, _ = chips(way)
    return lax.all_to_all(blocks, name, 0, 0, axis_index_groups=groups, tiled=False)


def copies(part, way):
    return jnp.broadcast_to(part[None], (chips(way)[2],) + part.shape)


def gather(part, way):
    return exchange(copies(part, way), way)


def swap(part):
    return lax.ppermute(part, "col", [(i, i ^ 1) for i in range(Y * CORES)])


def join(own, other):
    first = lax.axis_index("col") % CORES == 0
    return jnp.concatenate([jnp.where(first, own, other), jnp.where(first, other, own)], axis=0)


def split(value):
    high = value.astype(jnp.bfloat16)
    return high, (value - high.astype(jnp.float32)).astype(jnp.bfloat16)


def dot3(first, second, over):
    one = lambda a, b: lax.dot_general(
        a, b, ((over[:1], over[1:]), ((), ())), preferred_element_type=jnp.float32
    )
    return one(first[0], second[0]) + (one(first[0], second[1]) + one(first[1], second[0]))


def left_kernel(half_ref, basis_ref, blended_ref, out_ref):
    half = out_ref.shape[0]
    rows = pl.ds(pl.multiple_of(half_ref[0] * half, half), half)
    out_ref[...] = dot3(split(basis_ref[rows, :]), split(blended_ref[...]), (1, 1))


def sum_kernel(blocks_ref, out_ref):
    for i in range(out_ref.shape[0]):
        out_ref[i] = sum(blocks_ref[member, i] for member in range(blocks_ref.shape[0]))


def sum_copies_kernel(blocks_ref, out_ref):
    members = range(blocks_ref.shape[0])
    total = sum(blocks_ref[member] for member in members)
    for member in members:
        out_ref[member] = total


def square(k):
    return pl.ds(k * BLOCK, BLOCK)


def products_kernel(core_ref, left_ref, blended_ref, out_ref):
    members, uppers = out_ref.shape[:2]
    deep = left_ref.shape[0] // (8 * members * uppers)
    lanes = blended_ref.shape[1] // BLOCK
    right = dot3(split(left_ref[...]), split(blended_ref[...]), (1, 0))
    for j in range(lanes):
        tiles = right[:, j * BLOCK : (j + 1) * BLOCK].reshape(members, uppers, deep, 8, BLOCK)
        for i in range(deep):
            out_ref[:, :, i * lanes + j] = tiles[:, :, i]

    def gram(blocks):
        found = [dot(left_ref[square(k), :], left_ref[square(l), :], (1, 1), HIGHEST) for k, l in blocks]
        found.append(jnp.zeros((BLOCK, BLOCK), jnp.float32))
        for t in range(len(found) // 2):
            pair = jnp.concatenate(found[2 * t : 2 * t + 2], axis=0)
            out_ref[:, :, deep * lanes + t] = pair.reshape(members, uppers, 8, BLOCK)

    pl.when(core_ref[0] == 0)(lambda: gram(CORE_BLOCKS[0]))
    pl.when(core_ref[0] != 0)(lambda: gram(CORE_BLOCKS[1]))


def copies_kernel(sums_ref, out_ref):
    members, rows, cols = out_ref.shape
    uppers = sums_ref.shape[0]
    deep, lanes = rows // (8 * uppers), cols // BLOCK
    for j in range(lanes):
        tiles = [sums_ref[:, i * lanes + j] for i in range(deep)]
        piece = jnp.stack(tiles, axis=1).reshape(rows, BLOCK)
        for member in range(members):
            out_ref[member, :, j * BLOCK : (j + 1) * BLOCK] = piece


def invert_block(block, pending):
    groups = BLOCK // 8
    sub = lax.broadcasted_iota(jnp.int32, (8, BLOCK), 0)
    lane = lax.broadcasted_iota(jnp.int32, (8, BLOCK), 1)
    work = [block[8 * q : 8 * q + 8, :] for q in range(groups)]
    side = [jnp.where(lane == sub + 8 * q, 1.0, 0.0).astype(jnp.float32) for q in range(groups)]
    out = []
    column = lambda q, c: jnp.broadcast_to(work[q][:, c : c + 1], (8, BLOCK))
    ahead = [column(0, j) for j in range(8)]
    for p in range(groups):
        if pending:
            pending.pop(0)()
        spread = {q: [column(q, 8 * p + j) for j in range(8)] for q in range(p + 1, groups)}
        spread[p] = ahead
        nearby = {q: [column(q, 8 * p + 8 + j) for j in range(8)] for q in (p, p + 1) if p + 1 < groups}
        pivots = jnp.ones((8, BLOCK), jnp.float32)
        for j in range(8):
            over = lambda part: jnp.broadcast_to(part[j : j + 1, :], (8, BLOCK))
            row = {k: over(spread[p][k]) for k in range(j, 8)}
            pivots = jnp.where(sub == j, row[j], pivots)
            inverse = 1.0 / row[j]
            row_work, row_side = over(work[p]), over(side[p])
            row_near = [over(part) for part in nearby[p]] if nearby else []
            for q in range(p, groups):
                times = spread[q][j] * inverse
                if q == p:
                    times = jnp.where(sub > j, times, 0.0)
                for k in range(j + 1, 8):
                    spread[q][k] = spread[q][k] - times * row[k]
                if q in nearby:
                    nearby[q] = [part - times * over_row for part, over_row in zip(nearby[q], row_near)]
                work[q] = work[q] - times * row_work
                side[q] = side[q] - times * row_side
        ahead = nearby.get(p + 1)
        out.append(side[p] * lax.rsqrt(pivots))
    return jnp.concatenate(out, axis=0)


def eliminate(work, finish):
    count = work.shape[0] // BLOCK
    span = lambda first, last: pl.ds(first * BLOCK, (last - first) * BLOCK)
    pending = []
    for k in range(count):
        inverse = invert_block(work[square(k), square(k)], pending)
        while pending:
            pending.pop(0)()
        work[square(k), square(k)] = inverse
        if k + 1 < count:
            near = dot(inverse, work[square(k), square(k + 1)], (1, 0), HIGHEST)
            work[square(k), square(k + 1)] = near
            work[square(k + 1), square(k + 1)] -= dot(near, near, (0, 0), HIGHEST)

        def row(first, last, k=k, inverse=inverse):
            at = (square(k), span(first, last))
            work[at] = dot(inverse, work[at], (1, 0), HIGHEST)

        def below(i, first, last, k=k):
            change = dot(work[square(k), square(i)], work[square(k), span(first, last)], (0, 0), HIGHEST)
            at = (square(i), span(first, last))
            work[at] = -change if first == k else work[at] - change

        if k + 2 < count:
            pending.append(functools.partial(row, k + 2, count))
        if k:
            pending.append(functools.partial(row, 0, k))
        pending.append(functools.partial(finish, k))
        for i in range(k + 1, count):
            right = max(i, k + 2)
            if right < count:
                pending.append(functools.partial(below, i, right, count))
            pending.append(functools.partial(below, i, k, k + 1))
            if k:
                pending.append(functools.partial(below, i, 0, k))
    while pending:
        pending.pop(0)()


def factor_kernel(
    core_ref, own_hbm, other_hbm, left_ref, out_hbm, ortho_hbm, own_ref, other_ref, work, ortho_ref, high, low, sems
):
    arrive = [
        pltpu.make_async_copy(own_hbm, own_ref, sems.at[0]),
        pltpu.make_async_copy(other_hbm, other_ref, sems.at[1]),
    ]
    for part in arrive:
        part.start()
    high[...], low[...] = split(left_ref[...])

    def place(parts):
        for part_ref, blocks in zip(parts, CORE_BLOCKS):
            half = part_ref.shape[0] // 2
            for i, (k, l) in enumerate(blocks):
                tiles = part_ref[i % 2 * half : (i % 2 + 1) * half, :, i // 2]
                work[square(k), square(l)] = tiles.reshape(BLOCK, BLOCK)

    for part in arrive:
        part.wait()
    pl.when(core_ref[0] == 0)(lambda: place((own_ref, other_ref)))
    pl.when(core_ref[0] != 0)(lambda: place((other_ref, own_ref)))
    leave = []

    def finish(k):
        at, upto = square(k), pl.ds(0, (k + 1) * BLOCK)
        leave.append(pltpu.make_async_copy(work.at[at, upto], out_hbm.at[at, upto], sems.at[2 + 2 * k]))
        leave[-1].start()
        ortho_ref[at, :] = dot3(split(work[at, upto]), (high[upto, :], low[upto, :]), (1, 0))
        leave.append(pltpu.make_async_copy(ortho_ref.at[at], ortho_hbm.at[at], sems.at[3 + 2 * k]))
        leave[-1].start()

    eliminate(work, finish)
    for part in leave:
        part.wait()


def right_kernel(inverse_hbm, raw_ref, right_hbm, squares_ref, inverse_ref, right_ref, arrive, leave):
    count = raw_ref.shape[0] // BLOCK
    lower = [(square(i), pl.ds(0, (i + 1) * BLOCK)) for i in range(count)]
    blocks = [
        pltpu.make_async_copy(inverse_hbm.at[at], inverse_ref.at[at], arrive.at[i]) for i, at in enumerate(lower)
    ]
    for block in blocks:
        block.start()
    raw = split(raw_ref[...])
    eye = lax.broadcasted_iota(jnp.int32, (BLOCK, BLOCK), 0) == lax.broadcasted_iota(jnp.int32, (BLOCK, BLOCK), 1)
    out = []
    for i in range(count):
        at, upto = square(i), (i + 1) * BLOCK
        blocks[i].wait()
        right = dot3(split(inverse_ref[at, :upto]), [part[:upto] for part in raw], (1, 0))
        right_ref[at, :] = right
        out.append(pltpu.make_async_copy(right_ref.at[at], right_hbm.at[at], leave.at[i]))
        out[-1].start()
        sums = jnp.sum(right * right, axis=1, keepdims=True)
        line = jnp.sum(jnp.where(eye, sums, 0.0), axis=0, keepdims=True)
        for peer in range(squares_ref.shape[0]):
            squares_ref[peer, pl.ds(i, 1), :] = line
    for block in out:
        block.wait()


def momentum_kernel(blended_ref, ortho_ref, right_ref, out_ref):
    out_ref[...] = blended_ref[...] - (1.0 - retain) * dot3(split(ortho_ref[...]), split(right_ref[...]), (0, 0))


def update_kernel(start_ref, squares_ref, ortho_ref, right_ref, update_hbm, basis_ref, scaled, update_ref, leave):
    scale = math.sqrt(ROWS * COLS / RANK)
    rank, width = ortho_ref.shape[0], basis_ref.shape[0]
    rows = jnp.sum(squares_ref[...], axis=0)
    factors = lax.rsqrt(rows + epsilon_norm)
    eye = lax.broadcasted_iota(jnp.int32, (BLOCK, BLOCK), 0) == lax.broadcasted_iota(jnp.int32, (BLOCK, BLOCK), 1)
    for i in range(rank // BLOCK):
        at = pl.ds(i * BLOCK, BLOCK)
        column = jnp.sum(jnp.where(eye, factors[i : i + 1, :], 0.0), axis=1, keepdims=True)
        scaled[at, :] = jnp.broadcast_to(column, (BLOCK, BLOCK))
    ortho = split(ortho_ref[...] * (scale * scaled[:, :1]))
    cols = right_ref.shape[1]
    cut = cols // BLOCK // 2 * BLOCK
    parts = []
    for i, at in enumerate((pl.ds(0, cut), pl.ds(cut, cols - cut))):
        update_ref[:, at] = dot3(ortho, split(right_ref[:, at]), (0, 0))
        parts.append(pltpu.make_async_copy(update_ref.at[:, at], update_hbm.at[:, at], leave.at[i]))
        parts[-1].start()
    own = pl.ds(pl.multiple_of(start_ref[0], width), width)
    basis_ref[...] = right_ref[own, :] * scaled[own, :1]
    for part in parts:
        part.wait()


VMEM = pl.BlockSpec(memory_space=pltpu.VMEM)
SMEM = pl.BlockSpec(memory_space=pltpu.SMEM)
HBM = pl.BlockSpec(memory_space=pltpu.HBM)


def call(kernel, name, shapes, flops, *operands, scratch=(), limit=10, takes=(), gives=()):
    return pl.pallas_call(
        kernel,
        out_shape=[
            pltpu.HBM(shape, jnp.float32) if i in gives else jax.ShapeDtypeStruct(shape, jnp.float32)
            for i, shape in enumerate(shapes)
        ],
        in_specs=[
            SMEM if operand.dtype == jnp.int32 else HBM if i in takes else VMEM for i, operand in enumerate(operands)
        ],
        out_specs=[HBM if i in gives else VMEM for i in range(len(shapes))],
        scratch_shapes=list(scratch),
        compiler_params=pltpu.CompilerParams(vmem_limit_bytes=limit * 2**20),
        cost_estimate=pl.CostEstimate(flops=flops, bytes_accessed=4 * 2**20, transcendentals=0),
        name=name,
    )(*[pltpu.with_memory_space_constraint(x, pltpu.HBM) if i in takes else x for i, x in enumerate(operands)])


def body(momentum, gradient, right_basis):
    cols, width = right_basis.shape
    rows = momentum.shape[0]
    rank = width * lax.axis_size("row")
    members, uppers = chips("wide")[2], chips("long")[2]
    core = (lax.axis_index("col") % CORES).astype(jnp.int32).reshape(1)
    with jax.named_scope("basis_gather"):
        basis = gather(gather(right_basis.T, "long"), "wide").reshape(rank, cols)
    blended = momentum + gradient.astype(jnp.float32)
    with jax.named_scope("left"):
        half = [(rank // CORES, rows)]
        (left_other,) = call(left_kernel, "left_other", half, 10**9, 1 - core, basis, blended)
        left_other = swap(left_other)
        (left_own,) = call(left_kernel, "left_own", half, 10**9, core, basis, blended)
        parts = exchange((left_own + left_other).reshape(Y, -1, rows), "y")
        (parts,) = call(sum_copies_kernel, "left_sum", [parts.shape], 10**6, parts)
        left_own = exchange(parts, "y").reshape(-1, rows)
        left = join(left_own, swap(left_own)).reshape(X, 2, uppers, width, rows)
        left = left.transpose(0, 2, 1, 3, 4).reshape(rank, rows)
    with jax.named_scope("sums"):
        tiles = width // 8 * (cols // BLOCK)
        per_core = (len(CORE_BLOCKS[0]) + 1) // 2
        shape = (members, uppers, tiles + per_core, 8, BLOCK)
        (sums,) = call(products_kernel, "products", [shape], 2 * 10**9, core, left, blended)
        sums = exchange(sums, "wide")
        (sums,) = call(sum_kernel, "wide_sum", [sums.shape[1:]], 10**6, sums)
        sums = exchange(sums, "long")
        (sums,) = call(sum_copies_kernel, "long_sum", [sums.shape], 10**6, sums)
        sums = exchange(sums, "long")
        gram_own = gather(sums[:, tiles:], "wide")
        (raw,) = call(copies_kernel, "copies", [(members, rank // members, cols)], 10**6, sums)
        gram_own, raw = lax.optimization_barrier((gram_own, raw))
        gram_other = swap(gram_own)
        right_raw = exchange(raw, "wide").reshape(rank, cols)
    with jax.named_scope("factor"):
        inverse, ortho = call(
            factor_kernel,
            "factor",
            [(rank, rank), (rank, rows)],
            2 * 10**9,
            core,
            gram_own,
            gram_other,
            left,
            scratch=[
                pltpu.VMEM(gram_own.shape, jnp.float32),
                pltpu.VMEM(gram_own.shape, jnp.float32),
                pltpu.VMEM((rank, rank), jnp.float32),
                pltpu.VMEM((rank, rows), jnp.float32),
                pltpu.VMEM((rank, rows), jnp.bfloat16),
                pltpu.VMEM((rank, rows), jnp.bfloat16),
                pltpu.SemaphoreType.DMA((2 + 2 * (rank // BLOCK),)),
            ],
            takes=(1, 2),
            gives=(0, 1),
        )
    with jax.named_scope("right"):
        right, squares = call(
            right_kernel,
            "right",
            [(rank, cols), (lax.axis_size("col"), rank // BLOCK, BLOCK)],
            2 * 10**9,
            inverse,
            right_raw,
            scratch=[
                pltpu.VMEM((rank, rank), jnp.float32),
                pltpu.VMEM((rank, cols), jnp.float32),
                pltpu.SemaphoreType.DMA((rank // BLOCK,)),
                pltpu.SemaphoreType.DMA((rank // BLOCK,)),
            ],
            limit=14,
            takes=(0,),
            gives=(0,),
        )
    with jax.named_scope("squares"):
        squares = lax.all_to_all(squares, "col", 0, 0, tiled=False)
    with jax.named_scope("outputs"):
        (new_momentum,) = call(momentum_kernel, "momentum", [(rows, cols)], 10**9, blended, ortho, right)
        start = (lax.axis_index("row") * width).astype(jnp.int32).reshape(1)
        shapes = [(rows, cols), (width, cols)]
        scratch = [pltpu.VMEM((rank, BLOCK), jnp.float32), pltpu.VMEM((rows, cols), jnp.float32)]
        scratch += [pltpu.SemaphoreType.DMA((2,))]
        update, new_basis = call(
            update_kernel, "update", shapes, 10**9, start, squares, ortho, right, scratch=scratch, gives=(0,)
        )
        new_basis = new_basis.T
    return (update, new_momentum, new_basis)


def solution(mesh):
    in_specs = (P("row", "col"), P("row", "col"), P("col", "row"))
    out_specs = (P("row", "col"), P("row", "col"), P("col", "row"))
    return jax.shard_map(body, mesh=mesh, in_specs=in_specs, out_specs=out_specs, check_vma=False)
```

```python
import functools
import math

import jax
import jax.numpy as jnp
from jax import lax
from jax.experimental import pallas as pl
from jax.experimental.pallas import tpu as pltpu
from jax.sharding import PartitionSpec as P

ROWS = 8192
COLS = 14336
RANK = 512
BLOCK = 128
X, Y, Z, CORES = 4, 8, 8, 2
CORE_BLOCKS = (
    ((0, 0), (0, 1), (0, 2), (0, 3), (1, 1)),
    ((1, 2), (1, 3), (2, 2), (2, 3), (3, 3)),
)


HIGHEST = lax.Precision.HIGHEST
epsilon_norm = 1e-06
retain = 0.7


def dot(first, second, over, precision):
    return lax.dot_general(
        first, second, ((over[:1], over[1:]), ((), ())), precision=precision, preferred_element_type=jnp.float32
    )


def chips(way):
    upper = Z // 2
    row = lambda x, high, low: (x * upper + high) * 2 + low
    if way == "wide":
        return "row", [[row(x, high, low) for x in range(X) for low in range(2)] for high in range(upper)], 2 * X
    if way == "long":
        return "row", [[row(x, high, low) for high in range(upper)] for x in range(X) for low in range(2)], upper
    return "col", [[y * CORES + core for y in range(Y)] for core in range(CORES)], Y


def exchange(blocks, way):
    name, groups, _ = chips(way)
    return lax.all_to_all(blocks, name, 0, 0, axis_index_groups=groups, tiled=False)


def copies(part, way):
    return jnp.broadcast_to(part[None], (chips(way)[2],) + part.shape)


def gather(part, way):
    return exchange(copies(part, way), way)


def swap(part):
    return lax.ppermute(part, "col", [(i, i ^ 1) for i in range(Y * CORES)])


def split(value):
    high = value.astype(jnp.bfloat16)
    return high, (value - high.astype(jnp.float32)).astype(jnp.bfloat16)


def dot3(first, second, over):
    one = lambda a, b: lax.dot_general(
        a, b, ((over[:1], over[1:]), ((), ())), preferred_element_type=jnp.float32
    )
    return one(first[0], second[0]) + (one(first[0], second[1]) + one(first[1], second[0]))


def left_kernel(half_ref, basis_ref, blended_ref, out_ref):
    half = out_ref.shape[0]
    rows = pl.ds(pl.multiple_of(half_ref[0] * half, half), half)
    out_ref[...] = dot3(split(basis_ref[rows, :]), split(blended_ref[...]), (1, 1))


def sum_kernel(blocks_ref, out_ref):
    for i in range(out_ref.shape[0]):
        out_ref[i] = sum(blocks_ref[member, i] for member in range(blocks_ref.shape[0]))


def sum_copies_kernel(blocks_ref, out_ref):
    members = range(blocks_ref.shape[0])
    total = sum(blocks_ref[member] for member in members)
    for member in members:
        out_ref[member] = total


def square(k):
    return pl.ds(k * BLOCK, BLOCK)


def natural(part):
    upper = Z // 2
    width = part.shape[0] // (X // CORES * Z)
    order = [(x * 2 + low) * upper + high for x in range(X // CORES) for high in range(upper) for low in range(2)]
    return jnp.concatenate([part[i * width : (i + 1) * width] for i in order], axis=0)


def store_tiles(out_ref, first, members, right):
    uppers = out_ref.shape[1]
    deep, lanes = right.shape[0] // (8 * members * uppers), right.shape[1] // BLOCK
    for j in range(lanes):
        tiles = right[:, j * BLOCK : (j + 1) * BLOCK].reshape(members, uppers, deep, 8, BLOCK)
        for i in range(deep):
            out_ref[pl.ds(first, members), :, i * lanes + j] = tiles[:, :, i]


def own_products_kernel(part_ref, blended_ref, out_ref, rows_ref):
    rows = natural(part_ref[...])
    rows_ref[...] = rows
    store_tiles(out_ref, 0, out_ref.shape[0], dot3(split(rows), split(blended_ref[...]), (1, 0)))


def products_kernel(core_ref, done_ref, rows_ref, part_ref, blended_ref, out_ref, left_ref):
    members, uppers, tiles = done_ref.shape[:3]
    half = rows_ref.shape[0]
    core = core_ref[0]
    own = pl.ds(pl.multiple_of(core * half, half), half)
    other = pl.ds(pl.multiple_of((1 - core) * half, half), half)
    rows = natural(part_ref[...])
    left_ref[own, :] = rows_ref[...]
    left_ref[other, :] = rows
    out_ref[pl.ds(core * members, members), :, pl.ds(0, tiles)] = done_ref[...]
    store_tiles(out_ref, (1 - core) * members, members, dot3(split(rows), split(blended_ref[...]), (1, 0)))

    def gram(blocks):
        found = [dot(left_ref[square(k), :], left_ref[square(l), :], (1, 1), HIGHEST) for k, l in blocks]
        found.append(jnp.zeros((BLOCK, BLOCK), jnp.float32))
        for t in range(len(found) // 2):
            pair = jnp.concatenate(found[2 * t : 2 * t + 2], axis=0)
            out_ref[:, :, tiles + t] = pair.reshape(CORES * members, uppers, 8, BLOCK)

    pl.when(core_ref[0] == 0)(lambda: gram(CORE_BLOCKS[0]))
    pl.when(core_ref[0] != 0)(lambda: gram(CORE_BLOCKS[1]))


def copies_kernel(sums_ref, out_ref):
    members, rows, cols = out_ref.shape
    uppers = sums_ref.shape[0]
    deep, lanes = rows // (8 * uppers), cols // BLOCK
    for j in range(lanes):
        tiles = [sums_ref[:, i * lanes + j] for i in range(deep)]
        piece = jnp.stack(tiles, axis=1).reshape(rows, BLOCK)
        for member in range(members):
            out_ref[member, :, j * BLOCK : (j + 1) * BLOCK] = piece


def invert_block(block, pending):
    groups = BLOCK // 8
    sub = lax.broadcasted_iota(jnp.int32, (8, BLOCK), 0)
    lane = lax.broadcasted_iota(jnp.int32, (8, BLOCK), 1)
    work = [block[8 * q : 8 * q + 8, :] for q in range(groups)]
    side = [jnp.where(lane == sub + 8 * q, 1.0, 0.0).astype(jnp.float32) for q in range(groups)]
    out = []
    column = lambda q, c: jnp.broadcast_to(work[q][:, c : c + 1], (8, BLOCK))
    ahead = [column(0, j) for j in range(8)]
    for p in range(groups):
        if pending:
            pending.pop(0)()
        spread = {q: [column(q, 8 * p + j) for j in range(8)] for q in range(p + 1, groups)}
        spread[p] = ahead
        nearby = {q: [column(q, 8 * p + 8 + j) for j in range(8)] for q in (p, p + 1) if p + 1 < groups}
        pivots = jnp.ones((8, BLOCK), jnp.float32)
        for j in range(8):
            over = lambda part: jnp.broadcast_to(part[j : j + 1, :], (8, BLOCK))
            row = {k: over(spread[p][k]) for k in range(j, 8)}
            pivots = jnp.where(sub == j, row[j], pivots)
            inverse = 1.0 / row[j]
            row_work, row_side = over(work[p]), over(side[p])
            row_near = [over(part) for part in nearby[p]] if nearby else []
            for q in range(p, groups):
                times = spread[q][j] * inverse
                if q == p:
                    times = jnp.where(sub > j, times, 0.0)
                for k in range(j + 1, 8):
                    spread[q][k] = spread[q][k] - times * row[k]
                if q in nearby:
                    nearby[q] = [part - times * over_row for part, over_row in zip(nearby[q], row_near)]
                work[q] = work[q] - times * row_work
                side[q] = side[q] - times * row_side
        ahead = nearby.get(p + 1)
        out.append(side[p] * lax.rsqrt(pivots))
    return jnp.concatenate(out, axis=0)


def eliminate(work, finish):
    count = work.shape[0] // BLOCK
    span = lambda first, last: pl.ds(first * BLOCK, (last - first) * BLOCK)
    pending = []
    for k in range(count):
        inverse = invert_block(work[square(k), square(k)], pending)
        while pending:
            pending.pop(0)()
        work[square(k), square(k)] = inverse
        if k + 1 < count:
            near = dot(inverse, work[square(k), square(k + 1)], (1, 0), HIGHEST)
            work[square(k), square(k + 1)] = near
            work[square(k + 1), square(k + 1)] -= dot(near, near, (0, 0), HIGHEST)

        def row(first, last, k=k, inverse=inverse):
            at = (square(k), span(first, last))
            work[at] = dot(inverse, work[at], (1, 0), HIGHEST)

        def below(i, first, last, k=k):
            change = dot(work[square(k), square(i)], work[square(k), span(first, last)], (0, 0), HIGHEST)
            at = (square(i), span(first, last))
            work[at] = -change if first == k else work[at] - change

        if k + 2 < count:
            pending.append(functools.partial(row, k + 2, count))
        if k:
            pending.append(functools.partial(row, 0, k))
        pending.append(functools.partial(finish, k))
        for i in range(k + 1, count):
            right = max(i, k + 2)
            if right < count:
                pending.append(functools.partial(below, i, right, count))
            pending.append(functools.partial(below, i, k, k + 1))
            if k:
                pending.append(functools.partial(below, i, 0, k))
    while pending:
        pending.pop(0)()


def factor_kernel(
    core_ref, own_hbm, other_hbm, left_ref, out_hbm, ortho_hbm, own_ref, other_ref, work, ortho_ref, high, low, sems
):
    arrive = [
        pltpu.make_async_copy(own_hbm, own_ref, sems.at[0]),
        pltpu.make_async_copy(other_hbm, other_ref, sems.at[1]),
    ]
    for part in arrive:
        part.start()
    high[...], low[...] = split(left_ref[...])

    def place(parts):
        for part_ref, blocks in zip(parts, CORE_BLOCKS):
            half = part_ref.shape[0] // 2
            for i, (k, l) in enumerate(blocks):
                tiles = part_ref[i % 2 * half : (i % 2 + 1) * half, :, i // 2]
                work[square(k), square(l)] = tiles.reshape(BLOCK, BLOCK)

    for part in arrive:
        part.wait()
    pl.when(core_ref[0] == 0)(lambda: place((own_ref, other_ref)))
    pl.when(core_ref[0] != 0)(lambda: place((other_ref, own_ref)))
    leave = []

    def finish(k):
        at, upto = square(k), pl.ds(0, (k + 1) * BLOCK)
        leave.append(pltpu.make_async_copy(work.at[at, upto], out_hbm.at[at, upto], sems.at[2 + 2 * k]))
        leave[-1].start()
        ortho_ref[at, :] = dot3(split(work[at, upto]), (high[upto, :], low[upto, :]), (1, 0))
        leave.append(pltpu.make_async_copy(ortho_ref.at[at], ortho_hbm.at[at], sems.at[3 + 2 * k]))
        leave[-1].start()

    eliminate(work, finish)
    for part in leave:
        part.wait()


def right_kernel(inverse_hbm, raw_ref, right_hbm, squares_ref, inverse_ref, right_ref, arrive, leave):
    count = raw_ref.shape[0] // BLOCK
    lower = [(square(i), pl.ds(0, (i + 1) * BLOCK)) for i in range(count)]
    blocks = [
        pltpu.make_async_copy(inverse_hbm.at[at], inverse_ref.at[at], arrive.at[i]) for i, at in enumerate(lower)
    ]
    for block in blocks:
        block.start()
    raw = split(raw_ref[...])
    for block in blocks:
        block.wait()
    eye = lax.broadcasted_iota(jnp.int32, (BLOCK, BLOCK), 0) == lax.broadcasted_iota(jnp.int32, (BLOCK, BLOCK), 1)
    out = []
    for i in range(count):
        at, upto = square(i), (i + 1) * BLOCK
        right = dot3(split(inverse_ref[at, :upto]), [part[:upto] for part in raw], (1, 0))
        right_ref[at, :] = right
        out.append(pltpu.make_async_copy(right_ref.at[at], right_hbm.at[at], leave.at[i]))
        out[-1].start()
        sums = jnp.sum(right * right, axis=1, keepdims=True)
        line = jnp.sum(jnp.where(eye, sums, 0.0), axis=0, keepdims=True)
        for peer in range(squares_ref.shape[0]):
            squares_ref[peer, pl.ds(i, 1), :] = line
    for block in out:
        block.wait()


def momentum_kernel(blended_ref, ortho_ref, right_ref, out_ref):
    out_ref[...] = blended_ref[...] - (1.0 - retain) * dot3(split(ortho_ref[...]), split(right_ref[...]), (0, 0))


def update_kernel(start_ref, squares_ref, ortho_ref, right_ref, update_ref, basis_ref, scaled):
    scale = math.sqrt(ROWS * COLS / RANK)
    rank, width = ortho_ref.shape[0], basis_ref.shape[0]
    rows = jnp.sum(squares_ref[...], axis=0)
    factors = lax.rsqrt(rows + epsilon_norm)
    eye = lax.broadcasted_iota(jnp.int32, (BLOCK, BLOCK), 0) == lax.broadcasted_iota(jnp.int32, (BLOCK, BLOCK), 1)
    for i in range(rank // BLOCK):
        at = pl.ds(i * BLOCK, BLOCK)
        column = jnp.sum(jnp.where(eye, factors[i : i + 1, :], 0.0), axis=1, keepdims=True)
        scaled[at, :] = jnp.broadcast_to(column, (BLOCK, BLOCK))
    ortho = ortho_ref[...] * (scale * scaled[:, :1])
    update_ref[...] = dot3(split(ortho), split(right_ref[...]), (0, 0))
    own = pl.ds(pl.multiple_of(start_ref[0], width), width)
    basis_ref[...] = right_ref[own, :] * scaled[own, :1]


VMEM = pl.BlockSpec(memory_space=pltpu.VMEM)
SMEM = pl.BlockSpec(memory_space=pltpu.SMEM)
HBM = pl.BlockSpec(memory_space=pltpu.HBM)


def call(kernel, name, shapes, flops, *operands, scratch=(), limit=10, takes=(), gives=()):
    return pl.pallas_call(
        kernel,
        out_shape=[
            pltpu.HBM(shape, jnp.float32) if i in gives else jax.ShapeDtypeStruct(shape, jnp.float32)
            for i, shape in enumerate(shapes)
        ],
        in_specs=[
            SMEM if operand.dtype == jnp.int32 else HBM if i in takes else VMEM for i, operand in enumerate(operands)
        ],
        out_specs=[HBM if i in gives else VMEM for i in range(len(shapes))],
        scratch_shapes=list(scratch),
        compiler_params=pltpu.CompilerParams(vmem_limit_bytes=limit * 2**20),
        cost_estimate=pl.CostEstimate(flops=flops, bytes_accessed=4 * 2**20, transcendentals=0),
        name=name,
    )(*[pltpu.with_memory_space_constraint(x, pltpu.HBM) if i in takes else x for i, x in enumerate(operands)])


def body(momentum, gradient, right_basis):
    cols, width = right_basis.shape
    rows = momentum.shape[0]
    rank = width * lax.axis_size("row")
    members, uppers = chips("wide")[2], chips("long")[2]
    core = (lax.axis_index("col") % CORES).astype(jnp.int32).reshape(1)
    with jax.named_scope("basis_gather"):
        basis = gather(gather(right_basis.T, "long"), "wide").reshape(rank, cols)
    blended = momentum + gradient.astype(jnp.float32)
    with jax.named_scope("left"):
        half = [(rank // CORES, rows)]
        (left_other,) = call(left_kernel, "left_other", half, 10**9, 1 - core, basis, blended)
        left_other = swap(left_other)
        (left_own,) = call(left_kernel, "left_own", half, 10**9, core, basis, blended)
        parts = exchange((left_own + left_other).reshape(Y, -1, rows), "y")
        (parts,) = call(sum_copies_kernel, "left_sum", [parts.shape], 10**6, parts)
        left_own = exchange(parts, "y").reshape(-1, rows)
    with jax.named_scope("sums"):
        tiles = width // 8 * (cols // BLOCK)
        per_core = (len(CORE_BLOCKS[0]) + 1) // 2
        shape = (members, uppers, tiles + per_core, 8, BLOCK)
        mine = [(members // CORES, uppers, tiles, 8, BLOCK), (rank // CORES, rows)]
        left_other = swap(left_own)
        mine = call(own_products_kernel, "own_products", mine, 10**9, left_own, blended)
        shapes = [shape, (rank, rows)]
        sums, left = call(products_kernel, "products", shapes, 2 * 10**9, core, *mine, left_other, blended)
        sums = exchange(sums, "wide")
        (sums,) = call(sum_kernel, "wide_sum", [sums.shape[1:]], 10**6, sums)
        sums = exchange(sums, "long")
        (sums,) = call(sum_copies_kernel, "long_sum", [sums.shape], 10**6, sums)
        sums = exchange(sums, "long")
        gram_own = gather(sums[:, tiles:], "wide")
        (raw,) = call(copies_kernel, "copies", [(members, rank // members, cols)], 10**6, sums)
        gram_own, raw = lax.optimization_barrier((gram_own, raw))
        gram_other = swap(gram_own)
        right_raw = exchange(raw, "wide").reshape(rank, cols)
    with jax.named_scope("factor"):
        inverse, ortho = call(
            factor_kernel,
            "factor",
            [(rank, rank), (rank, rows)],
            2 * 10**9,
            core,
            gram_own,
            gram_other,
            left,
            scratch=[
                pltpu.VMEM(gram_own.shape, jnp.float32),
                pltpu.VMEM(gram_own.shape, jnp.float32),
                pltpu.VMEM((rank, rank), jnp.float32),
                pltpu.VMEM((rank, rows), jnp.float32),
                pltpu.VMEM((rank, rows), jnp.bfloat16),
                pltpu.VMEM((rank, rows), jnp.bfloat16),
                pltpu.SemaphoreType.DMA((2 + 2 * (rank // BLOCK),)),
            ],
            takes=(1, 2),
            gives=(0, 1),
        )
    with jax.named_scope("right"):
        right, squares = call(
            right_kernel,
            "right",
            [(rank, cols), (lax.axis_size("col"), rank // BLOCK, BLOCK)],
            2 * 10**9,
            inverse,
            right_raw,
            scratch=[
                pltpu.VMEM((rank, rank), jnp.float32),
                pltpu.VMEM((rank, cols), jnp.float32),
                pltpu.SemaphoreType.DMA((rank // BLOCK,)),
                pltpu.SemaphoreType.DMA((rank // BLOCK,)),
            ],
            limit=14,
            takes=(0,),
            gives=(0,),
        )
    with jax.named_scope("squares"):
        squares = lax.all_to_all(squares, "col", 0, 0, tiled=False)
    with jax.named_scope("outputs"):
        (new_momentum,) = call(momentum_kernel, "momentum", [(rows, cols)], 10**9, blended, ortho, right)
        start = (lax.axis_index("row") * width).astype(jnp.int32).reshape(1)
        shapes = [(rows, cols), (width, cols)]
        scratch = [pltpu.VMEM((rank, BLOCK), jnp.float32)]
        update, new_basis = call(
            update_kernel, "update", shapes, 10**9, start, squares, ortho, right, scratch=scratch
        )
        new_basis = new_basis.T
    return (update, new_momentum, new_basis)


def solution(mesh):
    in_specs = (P("row", "col"), P("row", "col"), P("col", "row"))
    out_specs = (P("row", "col"), P("row", "col"), P("col", "row"))
    return jax.shard_map(body, mesh=mesh, in_specs=in_specs, out_specs=out_specs, check_vma=False)
```

```python
import functools
import math

import jax
import jax.numpy as jnp
from jax import lax
from jax.experimental import pallas as pl
from jax.experimental.pallas import tpu as pltpu
from jax.sharding import PartitionSpec as P

ROWS = 8192
COLS = 14336
RANK = 512
BLOCK = 128
X, Y, Z, CORES = 4, 8, 8, 2
CORE_BLOCKS = (
    ((0, 0), (0, 1), (1, 1), (0, 2), (0, 3)),
    ((2, 2), (2, 3), (3, 3), (1, 2), (1, 3)),
)


HIGHEST = lax.Precision.HIGHEST
epsilon_norm = 1e-06
retain = 0.7


def dot(first, second, over, precision):
    return lax.dot_general(
        first, second, ((over[:1], over[1:]), ((), ())), precision=precision, preferred_element_type=jnp.float32
    )


def chips(way):
    upper = Z // 2
    row = lambda x, high, low: (x * upper + high) * 2 + low
    if way == "wide":
        return "row", [[row(x, high, low) for x in range(X) for low in range(2)] for high in range(upper)], 2 * X
    if way == "long":
        return "row", [[row(x, high, low) for high in range(upper)] for x in range(X) for low in range(2)], upper
    return "col", [[y * CORES + core for y in range(Y)] for core in range(CORES)], Y


def exchange(blocks, way):
    name, groups, _ = chips(way)
    return lax.all_to_all(blocks, name, 0, 0, axis_index_groups=groups, tiled=False)


def copies(part, way):
    return jnp.broadcast_to(part[None], (chips(way)[2],) + part.shape)


def gather(part, way):
    return exchange(copies(part, way), way)


def swap(part):
    return lax.ppermute(part, "col", [(i, i ^ 1) for i in range(Y * CORES)])


def split(value):
    high = value.astype(jnp.bfloat16)
    return high, (value - high.astype(jnp.float32)).astype(jnp.bfloat16)


def dot3(first, second, over):
    one = lambda a, b: lax.dot_general(
        a, b, ((over[:1], over[1:]), ((), ())), preferred_element_type=jnp.float32
    )
    return one(first[0], second[0]) + (one(first[0], second[1]) + one(first[1], second[0]))


def left_kernel(half_ref, basis_ref, blended_ref, out_ref):
    half = out_ref.shape[0]
    rows = pl.ds(pl.multiple_of(half_ref[0] * half, half), half)
    out_ref[...] = dot3(split(basis_ref[rows, :]), split(blended_ref[...]), (1, 1))


def sum_kernel(blocks_ref, out_ref):
    for i in range(out_ref.shape[0]):
        out_ref[i] = sum(blocks_ref[member, i] for member in range(blocks_ref.shape[0]))


def sum_copies_kernel(blocks_ref, out_ref):
    members = range(blocks_ref.shape[0])
    total = sum(blocks_ref[member] for member in members)
    for member in members:
        out_ref[member] = total


def square(k):
    return pl.ds(k * BLOCK if isinstance(k, int) else pl.multiple_of(k * BLOCK, BLOCK), BLOCK)


def natural(part):
    upper = Z // 2
    width = part.shape[0] // (X // CORES * Z)
    order = [(x * 2 + low) * upper + high for x in range(X // CORES) for high in range(upper) for low in range(2)]
    return jnp.concatenate([part[i * width : (i + 1) * width] for i in order], axis=0)


def store_tiles(out_ref, first, members, right):
    uppers = out_ref.shape[1]
    deep, lanes = right.shape[0] // (8 * members * uppers), right.shape[1] // BLOCK
    for j in range(lanes):
        tiles = right[:, j * BLOCK : (j + 1) * BLOCK].reshape(members, uppers, deep, 8, BLOCK)
        for i in range(deep):
            out_ref[pl.ds(first, members), :, i * lanes + j] = tiles[:, :, i]


def own_products_kernel(part_ref, blended_ref, out_ref, rows_ref, gram_ref):
    rows = natural(part_ref[...])
    rows_ref[...] = rows
    store_tiles(out_ref, 0, out_ref.shape[0], dot3(split(rows), split(blended_ref[...]), (1, 0)))
    for i, (k, l) in enumerate(CORE_BLOCKS[0][:3]):
        first, second = rows[k * BLOCK : (k + 1) * BLOCK], rows[l * BLOCK : (l + 1) * BLOCK]
        gram_ref[i] = dot(first, second, (1, 1), HIGHEST)


def products_kernel(core_ref, done_ref, rows_ref, gram_ref, part_ref, blended_ref, out_ref, left_ref):
    members, uppers, tiles = done_ref.shape[:3]
    half = rows_ref.shape[0]
    core = core_ref[0]
    own = pl.ds(pl.multiple_of(core * half, half), half)
    other = pl.ds(pl.multiple_of((1 - core) * half, half), half)
    rows = natural(part_ref[...])
    left_ref[own, :] = rows_ref[...]
    left_ref[other, :] = rows
    out_ref[pl.ds(core * members, members), :, pl.ds(0, tiles)] = done_ref[...]
    store_tiles(out_ref, (1 - core) * members, members, dot3(split(rows), split(blended_ref[...]), (1, 0)))
    across = dot(left_ref[square(core), :], left_ref[half:, :], (1, 1), HIGHEST)
    found = [gram_ref[i] for i in range(3)] + [across[:, :BLOCK], across[:, BLOCK:], jnp.zeros_like(gram_ref[0])]
    for t in range(len(found) // 2):
        pair = jnp.concatenate(found[2 * t : 2 * t + 2], axis=0)
        out_ref[:, :, tiles + t] = pair.reshape(CORES * members, uppers, 8, BLOCK)


def copies_kernel(sums_ref, out_ref):
    members, rows, cols = out_ref.shape
    uppers = sums_ref.shape[0]
    deep, lanes = rows // (8 * uppers), cols // BLOCK
    for j in range(lanes):
        tiles = [sums_ref[:, i * lanes + j] for i in range(deep)]
        piece = jnp.stack(tiles, axis=1).reshape(rows, BLOCK)
        for member in range(members):
            out_ref[member, :, j * BLOCK : (j + 1) * BLOCK] = piece


def invert_block(block, pending):
    groups = BLOCK // 8
    sub = lax.broadcasted_iota(jnp.int32, (8, BLOCK), 0)
    lane = lax.broadcasted_iota(jnp.int32, (8, BLOCK), 1)
    work = [block[8 * q : 8 * q + 8, :] for q in range(groups)]
    side = [jnp.where(lane == sub + 8 * q, 1.0, 0.0).astype(jnp.float32) for q in range(groups)]
    out = []
    column = lambda q, c: jnp.broadcast_to(work[q][:, c : c + 1], (8, BLOCK))
    ahead = [column(0, j) for j in range(8)]
    for p in range(groups):
        if pending:
            pending.pop(0)()
        spread = {q: [column(q, 8 * p + j) for j in range(8)] for q in range(p + 1, groups)}
        spread[p] = ahead
        nearby = {q: [column(q, 8 * p + 8 + j) for j in range(8)] for q in (p, p + 1) if p + 1 < groups}
        pivots = jnp.ones((8, BLOCK), jnp.float32)
        for j in range(8):
            over = lambda part: jnp.broadcast_to(part[j : j + 1, :], (8, BLOCK))
            row = {k: over(spread[p][k]) for k in range(j, 8)}
            pivots = jnp.where(sub == j, row[j], pivots)
            inverse = 1.0 / row[j]
            row_work, row_side = over(work[p]), over(side[p])
            row_near = [over(part) for part in nearby[p]] if nearby else []
            for q in range(p, groups):
                times = spread[q][j] * inverse
                if q == p:
                    times = jnp.where(sub > j, times, 0.0)
                for k in range(j + 1, 8):
                    spread[q][k] = spread[q][k] - times * row[k]
                if q in nearby:
                    nearby[q] = [part - times * over_row for part, over_row in zip(nearby[q], row_near)]
                work[q] = work[q] - times * row_work
                side[q] = side[q] - times * row_side
        ahead = nearby.get(p + 1)
        out.append(side[p] * lax.rsqrt(pivots))
    return jnp.concatenate(out, axis=0)


def eliminate(work, finish):
    count = work.shape[0] // BLOCK
    span = lambda first, last: pl.ds(first * BLOCK, (last - first) * BLOCK)
    pending = []
    for k in range(count):
        inverse = invert_block(work[square(k), square(k)], pending)
        while pending:
            pending.pop(0)()
        work[square(k), square(k)] = inverse
        if k + 1 < count:
            near = dot(inverse, work[square(k), square(k + 1)], (1, 0), HIGHEST)
            work[square(k), square(k + 1)] = near
            work[square(k + 1), square(k + 1)] -= dot(near, near, (0, 0), HIGHEST)

        def row(first, last, k=k, inverse=inverse):
            at = (square(k), span(first, last))
            work[at] = dot(inverse, work[at], (1, 0), HIGHEST)

        def below(i, first, last, k=k):
            change = dot(work[square(k), square(i)], work[square(k), span(first, last)], (0, 0), HIGHEST)
            at = (square(i), span(first, last))
            work[at] = -change if first == k else work[at] - change

        if k + 2 < count:
            pending.append(functools.partial(row, k + 2, count))
        if k:
            pending.append(functools.partial(row, 0, k))
        pending.append(functools.partial(finish, k))
        for i in range(k + 1, count):
            right = max(i, k + 2)
            if right < count:
                pending.append(functools.partial(below, i, right, count))
            pending.append(functools.partial(below, i, k, k + 1))
            if k:
                pending.append(functools.partial(below, i, 0, k))
    while pending:
        pending.pop(0)()


def factor_kernel(
    core_ref, own_hbm, other_hbm, left_ref, out_hbm, ortho_hbm, own_ref, other_ref, work, ortho_ref, high, low, sems
):
    arrive = [
        pltpu.make_async_copy(own_hbm, own_ref, sems.at[0]),
        pltpu.make_async_copy(other_hbm, other_ref, sems.at[1]),
    ]
    for part in arrive:
        part.start()
    high[...], low[...] = split(left_ref[...])

    def place(parts):
        for part_ref, blocks in zip(parts, CORE_BLOCKS):
            half = part_ref.shape[0] // 2
            for i, (k, l) in enumerate(blocks):
                tiles = part_ref[i % 2 * half : (i % 2 + 1) * half, :, i // 2]
                work[square(k), square(l)] = tiles.reshape(BLOCK, BLOCK)

    for part in arrive:
        part.wait()
    pl.when(core_ref[0] == 0)(lambda: place((own_ref, other_ref)))
    pl.when(core_ref[0] != 0)(lambda: place((other_ref, own_ref)))
    leave = []

    def finish(k):
        at, upto = square(k), pl.ds(0, (k + 1) * BLOCK)
        leave.append(pltpu.make_async_copy(work.at[at, upto], out_hbm.at[at, upto], sems.at[2 + 2 * k]))
        leave[-1].start()
        ortho_ref[at, :] = dot3(split(work[at, upto]), (high[upto, :], low[upto, :]), (1, 0))
        leave.append(pltpu.make_async_copy(ortho_ref.at[at], ortho_hbm.at[at], sems.at[3 + 2 * k]))
        leave[-1].start()

    eliminate(work, finish)
    for part in leave:
        part.wait()


def right_kernel(inverse_hbm, raw_ref, right_hbm, squares_ref, inverse_ref, right_ref, arrive, leave):
    count = raw_ref.shape[0] // BLOCK
    lower = [(square(i), pl.ds(0, (i + 1) * BLOCK)) for i in range(count)]
    blocks = [
        pltpu.make_async_copy(inverse_hbm.at[at], inverse_ref.at[at], arrive.at[i]) for i, at in enumerate(lower)
    ]
    for block in blocks:
        block.start()
    raw = split(raw_ref[...])
    for block in blocks:
        block.wait()
    eye = lax.broadcasted_iota(jnp.int32, (BLOCK, BLOCK), 0) == lax.broadcasted_iota(jnp.int32, (BLOCK, BLOCK), 1)
    out = []
    for i in range(count):
        at, upto = square(i), (i + 1) * BLOCK
        right = dot3(split(inverse_ref[at, :upto]), [part[:upto] for part in raw], (1, 0))
        right_ref[at, :] = right
        out.append(pltpu.make_async_copy(right_ref.at[at], right_hbm.at[at], leave.at[i]))
        out[-1].start()
        sums = jnp.sum(right * right, axis=1, keepdims=True)
        line = jnp.sum(jnp.where(eye, sums, 0.0), axis=0, keepdims=True)
        for peer in range(squares_ref.shape[0]):
            squares_ref[peer, pl.ds(i, 1), :] = line
    for block in out:
        block.wait()


def momentum_kernel(blended_ref, ortho_ref, right_ref, out_ref):
    out_ref[...] = blended_ref[...] - (1.0 - retain) * dot3(split(ortho_ref[...]), split(right_ref[...]), (0, 0))


def update_kernel(start_ref, squares_ref, ortho_ref, right_ref, update_ref, basis_ref, scaled):
    scale = math.sqrt(ROWS * COLS / RANK)
    rank, width = ortho_ref.shape[0], basis_ref.shape[0]
    rows = jnp.sum(squares_ref[...], axis=0)
    factors = lax.rsqrt(rows + epsilon_norm)
    eye = lax.broadcasted_iota(jnp.int32, (BLOCK, BLOCK), 0) == lax.broadcasted_iota(jnp.int32, (BLOCK, BLOCK), 1)
    for i in range(rank // BLOCK):
        at = pl.ds(i * BLOCK, BLOCK)
        column = jnp.sum(jnp.where(eye, factors[i : i + 1, :], 0.0), axis=1, keepdims=True)
        scaled[at, :] = jnp.broadcast_to(column, (BLOCK, BLOCK))
    ortho = ortho_ref[...] * (scale * scaled[:, :1])
    update_ref[...] = dot3(split(ortho), split(right_ref[...]), (0, 0))
    own = pl.ds(pl.multiple_of(start_ref[0], width), width)
    basis_ref[...] = right_ref[own, :] * scaled[own, :1]


VMEM = pl.BlockSpec(memory_space=pltpu.VMEM)
SMEM = pl.BlockSpec(memory_space=pltpu.SMEM)
HBM = pl.BlockSpec(memory_space=pltpu.HBM)


def call(kernel, name, shapes, flops, *operands, scratch=(), limit=10, takes=(), gives=()):
    return pl.pallas_call(
        kernel,
        out_shape=[
            pltpu.HBM(shape, jnp.float32) if i in gives else jax.ShapeDtypeStruct(shape, jnp.float32)
            for i, shape in enumerate(shapes)
        ],
        in_specs=[
            SMEM if operand.dtype == jnp.int32 else HBM if i in takes else VMEM for i, operand in enumerate(operands)
        ],
        out_specs=[HBM if i in gives else VMEM for i in range(len(shapes))],
        scratch_shapes=list(scratch),
        compiler_params=pltpu.CompilerParams(vmem_limit_bytes=limit * 2**20),
        cost_estimate=pl.CostEstimate(flops=flops, bytes_accessed=4 * 2**20, transcendentals=0),
        name=name,
    )(*[pltpu.with_memory_space_constraint(x, pltpu.HBM) if i in takes else x for i, x in enumerate(operands)])


def body(momentum, gradient, right_basis):
    cols, width = right_basis.shape
    rows = momentum.shape[0]
    rank = width * lax.axis_size("row")
    members, uppers = chips("wide")[2], chips("long")[2]
    core = (lax.axis_index("col") % CORES).astype(jnp.int32).reshape(1)
    with jax.named_scope("basis_gather"):
        basis = gather(gather(right_basis.T, "long"), "wide").reshape(rank, cols)
    blended = momentum + gradient.astype(jnp.float32)
    with jax.named_scope("left"):
        half = [(rank // CORES, rows)]
        (left_other,) = call(left_kernel, "left_other", half, 10**9, 1 - core, basis, blended)
        left_other = swap(left_other)
        (left_own,) = call(left_kernel, "left_own", half, 10**9, core, basis, blended)
        parts = exchange((left_own + left_other).reshape(Y, -1, rows), "y")
        (parts,) = call(sum_copies_kernel, "left_sum", [parts.shape], 10**6, parts)
        left_own = exchange(parts, "y").reshape(-1, rows)
    with jax.named_scope("sums"):
        tiles = width // 8 * (cols // BLOCK)
        per_core = (len(CORE_BLOCKS[0]) + 1) // 2
        shape = (members, uppers, tiles + per_core, 8, BLOCK)
        mine = [(members // CORES, uppers, tiles, 8, BLOCK), (rank // CORES, rows), (3, BLOCK, BLOCK)]
        left_other = swap(left_own)
        mine = call(own_products_kernel, "own_products", mine, 10**9, left_own, blended)
        shapes = [shape, (rank, rows)]
        sums, left = call(products_kernel, "products", shapes, 2 * 10**9, core, *mine, left_other, blended)
        sums = exchange(sums, "wide")
        (sums,) = call(sum_kernel, "wide_sum", [sums.shape[1:]], 10**6, sums)
        sums = exchange(sums, "long")
        (sums,) = call(sum_copies_kernel, "long_sum", [sums.shape], 10**6, sums)
        sums = exchange(sums, "long")
        gram_own = gather(sums[:, tiles:], "wide")
        (raw,) = call(copies_kernel, "copies", [(members, rank // members, cols)], 10**6, sums)
        gram_own, raw = lax.optimization_barrier((gram_own, raw))
        gram_other = swap(gram_own)
        right_raw = exchange(raw, "wide").reshape(rank, cols)
    with jax.named_scope("factor"):
        inverse, ortho = call(
            factor_kernel,
            "factor",
            [(rank, rank), (rank, rows)],
            2 * 10**9,
            core,
            gram_own,
            gram_other,
            left,
            scratch=[
                pltpu.VMEM(gram_own.shape, jnp.float32),
                pltpu.VMEM(gram_own.shape, jnp.float32),
                pltpu.VMEM((rank, rank), jnp.float32),
                pltpu.VMEM((rank, rows), jnp.float32),
                pltpu.VMEM((rank, rows), jnp.bfloat16),
                pltpu.VMEM((rank, rows), jnp.bfloat16),
                pltpu.SemaphoreType.DMA((2 + 2 * (rank // BLOCK),)),
            ],
            takes=(1, 2),
            gives=(0, 1),
        )
    with jax.named_scope("right"):
        right, squares = call(
            right_kernel,
            "right",
            [(rank, cols), (lax.axis_size("col"), rank // BLOCK, BLOCK)],
            2 * 10**9,
            inverse,
            right_raw,
            scratch=[
                pltpu.VMEM((rank, rank), jnp.float32),
                pltpu.VMEM((rank, cols), jnp.float32),
                pltpu.SemaphoreType.DMA((rank // BLOCK,)),
                pltpu.SemaphoreType.DMA((rank // BLOCK,)),
            ],
            limit=14,
            takes=(0,),
            gives=(0,),
        )
    with jax.named_scope("squares"):
        squares = lax.all_to_all(squares, "col", 0, 0, tiled=False)
    with jax.named_scope("outputs"):
        (new_momentum,) = call(momentum_kernel, "momentum", [(rows, cols)], 10**9, blended, ortho, right)
        start = (lax.axis_index("row") * width).astype(jnp.int32).reshape(1)
        shapes = [(rows, cols), (width, cols)]
        scratch = [pltpu.VMEM((rank, BLOCK), jnp.float32)]
        update, new_basis = call(
            update_kernel, "update", shapes, 10**9, start, squares, ortho, right, scratch=scratch
        )
        new_basis = new_basis.T
    return (update, new_momentum, new_basis)


def solution(mesh):
    in_specs = (P("row", "col"), P("row", "col"), P("col", "row"))
    out_specs = (P("row", "col"), P("row", "col"), P("col", "row"))
    return jax.shard_map(body, mesh=mesh, in_specs=in_specs, out_specs=out_specs, check_vma=False)
```

```python
import functools
import math

import jax
import jax.numpy as jnp
from jax import lax
from jax.experimental import pallas as pl
from jax.experimental.pallas import tpu as pltpu
from jax.sharding import PartitionSpec as P

ROWS = 8192
COLS = 14336
RANK = 512
BLOCK = 128
X, Y, Z, CORES = 4, 8, 8, 2
CORE_BLOCKS = (
    ((0, 0), (0, 1), (1, 1), (0, 2), (0, 3)),
    ((2, 2), (2, 3), (3, 3), (1, 2), (1, 3)),
)


HIGHEST = lax.Precision.HIGHEST
epsilon_norm = 1e-06
retain = 0.7


def dot(first, second, over, precision):
    return lax.dot_general(
        first, second, ((over[:1], over[1:]), ((), ())), precision=precision, preferred_element_type=jnp.float32
    )


def chips(way):
    upper = Z // 2
    row = lambda x, high, low: (x * upper + high) * 2 + low
    if way == "wide":
        return "row", [[row(x, high, low) for x in range(X) for low in range(2)] for high in range(upper)], 2 * X
    if way == "long":
        return "row", [[row(x, high, low) for high in range(upper)] for x in range(X) for low in range(2)], upper
    return "col", [[y * CORES + core for y in range(Y)] for core in range(CORES)], Y


def exchange(blocks, way):
    name, groups, _ = chips(way)
    return lax.all_to_all(blocks, name, 0, 0, axis_index_groups=groups, tiled=False)


def copies(part, way):
    return jnp.broadcast_to(part[None], (chips(way)[2],) + part.shape)


def gather(part, way):
    return exchange(copies(part, way), way)


def swap(part):
    return lax.ppermute(part, "col", [(i, i ^ 1) for i in range(Y * CORES)])


def split(value):
    high = value.astype(jnp.bfloat16)
    return high, (value - high.astype(jnp.float32)).astype(jnp.bfloat16)


def dot3(first, second, over):
    one = lambda a, b: lax.dot_general(
        a, b, ((over[:1], over[1:]), ((), ())), preferred_element_type=jnp.float32
    )
    return one(first[0], second[0]) + (one(first[0], second[1]) + one(first[1], second[0]))


def left_kernel(half_ref, basis_ref, blended_ref, out_ref):
    half = out_ref.shape[0]
    rows = pl.ds(pl.multiple_of(half_ref[0] * half, half), half)
    out_ref[...] = dot3(split(basis_ref[rows, :]), split(blended_ref[...]), (1, 1))


def sum_kernel(blocks_ref, out_ref):
    for i in range(out_ref.shape[0]):
        out_ref[i] = sum(blocks_ref[member, i] for member in range(blocks_ref.shape[0]))


def sum_copies_kernel(blocks_ref, out_ref):
    members = range(blocks_ref.shape[0])
    total = sum(blocks_ref[member] for member in members)
    for member in members:
        out_ref[member] = total


def square(k):
    return pl.ds(k * BLOCK if isinstance(k, int) else pl.multiple_of(k * BLOCK, BLOCK), BLOCK)


def natural(part):
    upper = Z // 2
    width = part.shape[0] // (X // CORES * Z)
    order = [(x * 2 + low) * upper + high for x in range(X // CORES) for high in range(upper) for low in range(2)]
    return jnp.concatenate([part[i * width : (i + 1) * width] for i in order], axis=0)


def store_tiles(out_ref, first, members, right):
    uppers = out_ref.shape[1]
    deep, lanes = right.shape[0] // (8 * members * uppers), right.shape[1] // BLOCK
    for j in range(lanes):
        tiles = right[:, j * BLOCK : (j + 1) * BLOCK].reshape(members, uppers, deep, 8, BLOCK)
        for i in range(deep):
            out_ref[pl.ds(first, members), :, i * lanes + j] = tiles[:, :, i]


def own_products_kernel(part_ref, blended_ref, out_ref, rows_ref, gram_ref):
    rows = natural(part_ref[...])
    rows_ref[...] = rows
    store_tiles(out_ref, 0, out_ref.shape[0], dot3(split(rows), split(blended_ref[...]), (1, 0)))
    for i, (k, l) in enumerate(CORE_BLOCKS[0][:3]):
        first, second = rows[k * BLOCK : (k + 1) * BLOCK], rows[l * BLOCK : (l + 1) * BLOCK]
        gram_ref[i] = dot(first, second, (1, 1), HIGHEST)


def products_kernel(core_ref, done_ref, rows_ref, gram_ref, part_ref, blended_ref, out_ref, left_ref):
    members, uppers, tiles = done_ref.shape[:3]
    half = rows_ref.shape[0]
    core = core_ref[0]
    own = pl.ds(pl.multiple_of(core * half, half), half)
    other = pl.ds(pl.multiple_of((1 - core) * half, half), half)
    rows = natural(part_ref[...])
    left_ref[own, :] = rows_ref[...]
    left_ref[other, :] = rows
    out_ref[pl.ds(core * members, members), :, pl.ds(0, tiles)] = done_ref[...]
    store_tiles(out_ref, (1 - core) * members, members, dot3(split(rows), split(blended_ref[...]), (1, 0)))
    across = dot(left_ref[square(core), :], left_ref[half:, :], (1, 1), HIGHEST)
    found = [gram_ref[i] for i in range(3)] + [across[:, :BLOCK], across[:, BLOCK:], jnp.zeros_like(gram_ref[0])]
    for t in range(len(found) // 2):
        pair = jnp.concatenate(found[2 * t : 2 * t + 2], axis=0)
        out_ref[:, :, tiles + t] = pair.reshape(CORES * members, uppers, 8, BLOCK)


def copies_kernel(sums_ref, out_ref):
    members, rows, cols = out_ref.shape
    uppers = sums_ref.shape[0]
    deep, lanes = rows // (8 * uppers), cols // BLOCK
    for j in range(lanes):
        tiles = [sums_ref[:, i * lanes + j] for i in range(deep)]
        piece = jnp.stack(tiles, axis=1).reshape(rows, BLOCK)
        for member in range(members):
            out_ref[member, :, j * BLOCK : (j + 1) * BLOCK] = piece


def invert_block(block, pending):
    groups = BLOCK // 8
    sub = lax.broadcasted_iota(jnp.int32, (8, BLOCK), 0)
    lane = lax.broadcasted_iota(jnp.int32, (8, BLOCK), 1)
    work = [block[8 * q : 8 * q + 8, :] for q in range(groups)]
    side = [jnp.where(lane == sub + 8 * q, 1.0, 0.0).astype(jnp.float32) for q in range(groups)]
    out = []
    column = lambda q, c: jnp.broadcast_to(work[q][:, c : c + 1], (8, BLOCK))
    ahead = [column(0, j) for j in range(8)]
    for p in range(groups):
        if pending:
            pending.pop(0)()
        spread = {q: [column(q, 8 * p + j) for j in range(8)] for q in range(p + 1, groups)}
        spread[p] = ahead
        nearby = {q: [column(q, 8 * p + 8 + j) for j in range(8)] for q in (p, p + 1) if p + 1 < groups}
        pivots = jnp.ones((8, BLOCK), jnp.float32)
        for j in range(8):
            over = lambda part: jnp.broadcast_to(part[j : j + 1, :], (8, BLOCK))
            row = {k: over(spread[p][k]) for k in range(j, 8)}
            pivots = jnp.where(sub == j, row[j], pivots)
            inverse = 1.0 / row[j]
            row_work, row_side = over(work[p]), over(side[p])
            row_near = [over(part) for part in nearby[p]] if nearby else []
            for q in range(p, groups):
                times = spread[q][j] * inverse
                if q == p:
                    times = jnp.where(sub > j, times, 0.0)
                for k in range(j + 1, 8):
                    spread[q][k] = spread[q][k] - times * row[k]
                if q in nearby:
                    nearby[q] = [part - times * over_row for part, over_row in zip(nearby[q], row_near)]
                work[q] = work[q] - times * row_work
                side[q] = side[q] - times * row_side
        ahead = nearby.get(p + 1)
        out.append(side[p] * lax.rsqrt(pivots))
    return jnp.concatenate(out, axis=0)


def eliminate(work, finish):
    count = work.shape[0] // BLOCK
    span = lambda first, last: pl.ds(first * BLOCK, (last - first) * BLOCK)
    pending = []
    for k in range(count):
        inverse = invert_block(work[square(k), square(k)], pending)
        while pending:
            pending.pop(0)()
        work[square(k), square(k)] = inverse
        if k + 1 < count:
            near = dot(inverse, work[square(k), square(k + 1)], (1, 0), HIGHEST)
            work[square(k), square(k + 1)] = near
            work[square(k + 1), square(k + 1)] -= dot(near, near, (0, 0), HIGHEST)

        def row(first, last, k=k, inverse=inverse):
            at = (square(k), span(first, last))
            work[at] = dot(inverse, work[at], (1, 0), HIGHEST)

        def below(i, first, last, k=k):
            change = dot(work[square(k), square(i)], work[square(k), span(first, last)], (0, 0), HIGHEST)
            at = (square(i), span(first, last))
            work[at] = -change if first == k else work[at] - change

        if k + 2 < count:
            pending.append(functools.partial(row, k + 2, count))
        if k:
            pending.append(functools.partial(row, 0, k))
        pending.append(functools.partial(finish, k))
        for i in range(k + 1, count):
            right = max(i, k + 2)
            if right < count:
                pending.append(functools.partial(below, i, right, count))
            pending.append(functools.partial(below, i, k, k + 1))
            if k:
                pending.append(functools.partial(below, i, 0, k))
    while pending:
        pending.pop(0)()


def factor_kernel(
    core_ref, own_hbm, other_hbm, left_ref, out_hbm, ortho_hbm, own_ref, other_ref, work, ortho_ref, high, low, sems
):
    arrive = [
        pltpu.make_async_copy(own_hbm, own_ref, sems.at[0]),
        pltpu.make_async_copy(other_hbm, other_ref, sems.at[1]),
    ]
    for part in arrive:
        part.start()
    high[...], low[...] = split(left_ref[...])

    core = core_ref[0]
    for part, part_ref, half in zip(arrive, (own_ref, other_ref), (core, 1 - core)):
        part.wait()
        for i, (k, l) in enumerate(CORE_BLOCKS[0]):
            members = part_ref.shape[0] // 2
            tiles = part_ref[i % 2 * members : (i % 2 + 1) * members, :, i // 2]
            at = (square(half * 2 + k), square(half * 2 + l)) if l < 2 else (square(half), square(l))
            work[at] = tiles.reshape(BLOCK, BLOCK)
    leave = []

    def finish(k):
        at, upto = square(k), pl.ds(0, (k + 1) * BLOCK)
        leave.append(pltpu.make_async_copy(work.at[at, upto], out_hbm.at[at, upto], sems.at[2 + 2 * k]))
        leave[-1].start()
        ortho_ref[at, :] = dot3(split(work[at, upto]), (high[upto, :], low[upto, :]), (1, 0))
        leave.append(pltpu.make_async_copy(ortho_ref.at[at], ortho_hbm.at[at], sems.at[3 + 2 * k]))
        leave[-1].start()

    eliminate(work, finish)
    for part in leave:
        part.wait()


def right_kernel(inverse_hbm, raw_ref, right_hbm, squares_ref, inverse_ref, right_ref, arrive, leave):
    count = raw_ref.shape[0] // BLOCK
    lower = [(square(i), pl.ds(0, (i + 1) * BLOCK)) for i in range(count)]
    blocks = [
        pltpu.make_async_copy(inverse_hbm.at[at], inverse_ref.at[at], arrive.at[i]) for i, at in enumerate(lower)
    ]
    for block in blocks:
        block.start()
    raw = split(raw_ref[...])
    for block in blocks:
        block.wait()
    eye = lax.broadcasted_iota(jnp.int32, (BLOCK, BLOCK), 0) == lax.broadcasted_iota(jnp.int32, (BLOCK, BLOCK), 1)
    out = []
    for i in range(count):
        at, upto = square(i), (i + 1) * BLOCK
        right = dot3(split(inverse_ref[at, :upto]), [part[:upto] for part in raw], (1, 0))
        right_ref[at, :] = right
        out.append(pltpu.make_async_copy(right_ref.at[at], right_hbm.at[at], leave.at[i]))
        out[-1].start()
        sums = jnp.sum(right * right, axis=1, keepdims=True)
        line = jnp.sum(jnp.where(eye, sums, 0.0), axis=0, keepdims=True)
        for peer in range(squares_ref.shape[0]):
            squares_ref[peer, pl.ds(i, 1), :] = line
    for block in out:
        block.wait()


def momentum_kernel(blended_ref, ortho_ref, right_ref, out_ref):
    out_ref[...] = blended_ref[...] - (1.0 - retain) * dot3(split(ortho_ref[...]), split(right_ref[...]), (0, 0))


def update_kernel(start_ref, squares_ref, ortho_ref, right_ref, update_ref, basis_ref, scaled):
    scale = math.sqrt(ROWS * COLS / RANK)
    rank, width = ortho_ref.shape[0], basis_ref.shape[0]
    rows = jnp.sum(squares_ref[...], axis=0)
    factors = lax.rsqrt(rows + epsilon_norm)
    eye = lax.broadcasted_iota(jnp.int32, (BLOCK, BLOCK), 0) == lax.broadcasted_iota(jnp.int32, (BLOCK, BLOCK), 1)
    for i in range(rank // BLOCK):
        at = pl.ds(i * BLOCK, BLOCK)
        column = jnp.sum(jnp.where(eye, factors[i : i + 1, :], 0.0), axis=1, keepdims=True)
        scaled[at, :] = jnp.broadcast_to(column, (BLOCK, BLOCK))
    ortho = ortho_ref[...] * (scale * scaled[:, :1])
    update_ref[...] = dot3(split(ortho), split(right_ref[...]), (0, 0))
    own = pl.ds(pl.multiple_of(start_ref[0], width), width)
    basis_ref[...] = right_ref[own, :] * scaled[own, :1]


VMEM = pl.BlockSpec(memory_space=pltpu.VMEM)
SMEM = pl.BlockSpec(memory_space=pltpu.SMEM)
HBM = pl.BlockSpec(memory_space=pltpu.HBM)


def call(kernel, name, shapes, flops, *operands, scratch=(), limit=10, takes=(), gives=()):
    return pl.pallas_call(
        kernel,
        out_shape=[
            pltpu.HBM(shape, jnp.float32) if i in gives else jax.ShapeDtypeStruct(shape, jnp.float32)
            for i, shape in enumerate(shapes)
        ],
        in_specs=[
            SMEM if operand.dtype == jnp.int32 else HBM if i in takes else VMEM for i, operand in enumerate(operands)
        ],
        out_specs=[HBM if i in gives else VMEM for i in range(len(shapes))],
        scratch_shapes=list(scratch),
        compiler_params=pltpu.CompilerParams(vmem_limit_bytes=limit * 2**20),
        cost_estimate=pl.CostEstimate(flops=flops, bytes_accessed=4 * 2**20, transcendentals=0),
        name=name,
    )(*[pltpu.with_memory_space_constraint(x, pltpu.HBM) if i in takes else x for i, x in enumerate(operands)])


def body(momentum, gradient, right_basis):
    cols, width = right_basis.shape
    rows = momentum.shape[0]
    rank = width * lax.axis_size("row")
    members, uppers = chips("wide")[2], chips("long")[2]
    core = (lax.axis_index("col") % CORES).astype(jnp.int32).reshape(1)
    with jax.named_scope("basis_gather"):
        basis = gather(gather(right_basis.T, "long"), "wide").reshape(rank, cols)
    blended = momentum + gradient.astype(jnp.float32)
    with jax.named_scope("left"):
        half = [(rank // CORES, rows)]
        (left_other,) = call(left_kernel, "left_other", half, 10**9, 1 - core, basis, blended)
        left_other = swap(left_other)
        (left_own,) = call(left_kernel, "left_own", half, 10**9, core, basis, blended)
        parts = exchange((left_own + left_other).reshape(Y, -1, rows), "y")
        (parts,) = call(sum_copies_kernel, "left_sum", [parts.shape], 10**6, parts)
        left_own = exchange(parts, "y").reshape(-1, rows)
    with jax.named_scope("sums"):
        tiles = width // 8 * (cols // BLOCK)
        per_core = (len(CORE_BLOCKS[0]) + 1) // 2
        shape = (members, uppers, tiles + per_core, 8, BLOCK)
        mine = [(members // CORES, uppers, tiles, 8, BLOCK), (rank // CORES, rows), (3, BLOCK, BLOCK)]
        left_other = swap(left_own)
        mine = call(own_products_kernel, "own_products", mine, 10**9, left_own, blended)
        shapes = [shape, (rank, rows)]
        sums, left = call(products_kernel, "products", shapes, 2 * 10**9, core, *mine, left_other, blended)
        sums = exchange(sums, "wide")
        (sums,) = call(sum_kernel, "wide_sum", [sums.shape[1:]], 10**6, sums)
        sums = exchange(sums, "long")
        (sums,) = call(sum_copies_kernel, "long_sum", [sums.shape], 10**6, sums)
        sums = exchange(sums, "long")
        gram_own = gather(sums[:, tiles:], "wide")
        (raw,) = call(copies_kernel, "copies", [(members, rank // members, cols)], 10**6, sums)
        gram_own, raw = lax.optimization_barrier((gram_own, raw))
        gram_other = swap(gram_own)
        right_raw = exchange(raw, "wide").reshape(rank, cols)
    with jax.named_scope("factor"):
        inverse, ortho = call(
            factor_kernel,
            "factor",
            [(rank, rank), (rank, rows)],
            2 * 10**9,
            core,
            gram_own,
            gram_other,
            left,
            scratch=[
                pltpu.VMEM(gram_own.shape, jnp.float32),
                pltpu.VMEM(gram_own.shape, jnp.float32),
                pltpu.VMEM((rank, rank), jnp.float32),
                pltpu.VMEM((rank, rows), jnp.float32),
                pltpu.VMEM((rank, rows), jnp.bfloat16),
                pltpu.VMEM((rank, rows), jnp.bfloat16),
                pltpu.SemaphoreType.DMA((2 + 2 * (rank // BLOCK),)),
            ],
            takes=(1, 2),
            gives=(0, 1),
        )
    with jax.named_scope("right"):
        right, squares = call(
            right_kernel,
            "right",
            [(rank, cols), (lax.axis_size("col"), rank // BLOCK, BLOCK)],
            2 * 10**9,
            inverse,
            right_raw,
            scratch=[
                pltpu.VMEM((rank, rank), jnp.float32),
                pltpu.VMEM((rank, cols), jnp.float32),
                pltpu.SemaphoreType.DMA((rank // BLOCK,)),
                pltpu.SemaphoreType.DMA((rank // BLOCK,)),
            ],
            limit=14,
            takes=(0,),
            gives=(0,),
        )
    with jax.named_scope("squares"):
        squares = lax.all_to_all(squares, "col", 0, 0, tiled=False)
    with jax.named_scope("outputs"):
        (new_momentum,) = call(momentum_kernel, "momentum", [(rows, cols)], 10**9, blended, ortho, right)
        start = (lax.axis_index("row") * width).astype(jnp.int32).reshape(1)
        shapes = [(rows, cols), (width, cols)]
        scratch = [pltpu.VMEM((rank, BLOCK), jnp.float32)]
        update, new_basis = call(
            update_kernel, "update", shapes, 10**9, start, squares, ortho, right, scratch=scratch
        )
        new_basis = new_basis.T
    return (update, new_momentum, new_basis)


def solution(mesh):
    in_specs = (P("row", "col"), P("row", "col"), P("col", "row"))
    out_specs = (P("row", "col"), P("row", "col"), P("col", "row"))
    return jax.shard_map(body, mesh=mesh, in_specs=in_specs, out_specs=out_specs, check_vma=False)
```
